256 devices in a mesh: seq: 32 (over x, z), dp: 8 (over y, core).
Axes of the slice: x: 4, y: 4, z: 8, core: 2. Of those that a mesh axis runs over, the one named last changes fastest.
Arguments:
- layer_input: bfloat16 [8, 4096, 4096], P('dp', 'seq'), may hold values from -6 to 6
- projection: bfloat16 [4096, 256], replicated, may hold values from -0.09375 to 0.09375
- ssm_input: bfloat16 [8, 4096, 4096], P('dp', 'seq'), may hold values from -6 to 6
- step_logit: float32 [8, 4096, 64], P('dp', 'seq'), may hold values from -4 to 4
- decay_rate: float32 [64], replicated, may hold values from 0.00012207031 to 0.1
- output_grad: bfloat16 [8, 4096, 4096], P('dp', 'seq'), may hold values from -6 to 6
Outputs:
- input_grad: bfloat16 [8, 4096, 4096], P('dp', 'seq')
- step_grad: float32 [8, 4096, 64], P('dp', 'seq')
- rate_grad: float32 [64], replicated
- projection_grad: float32 [4096, 256], P('seq')
The draws below stay inside these ranges and needn't reach their ends.
All inputs are finite; a program needn't handle non-finite values.
Results may differ from the reference program's by a relative error of at most 0.011.
Values sent between devices are 32-bit elements; how exact they have to be, the bound alone decides.
No kernel may reach another device: no remote copies, remote signals or barrier semaphores. Data moves between devices by JAX's collectives and lax.ppermute only.
A program may use at most 320 MiB of HBM per device.

```python
import math
import jax
import jax.numpy as jnp
from jax import lax

D = 4096
H = 64
P_SIZE = 64
N = 128
L_DEV = 128
HP = 4096
LENGTH = 4096
TRACES = 8


def shard_levels(stream_key, dims, split, smallest, high):
    level = 1.0
    for position, parts in split:
        heights = jax.random.uniform(jax.random.fold_in(jax.random.fold_in(stream_key, 6), position), (parts,), jnp.float32, smallest / len(split), high / len(split))
        level = level * jnp.repeat(jnp.exp(heights), dims[position] // parts).reshape((-1,) + (1,) * (len(dims) - 1 - position))
    return level


def bell_draw(own_key, shape, width, most, cuts=(), dtype=jnp.bfloat16):
    values = jax.random.normal(own_key, shape, jnp.float32) * width
    if len(cuts) > 0:
        values = shard_levels(own_key, shape, cuts, -0.22, 0.18) * values
    return jnp.clip(values, min=-most, max=most).astype(dtype)


def setup_inputs(seed: int = 0) -> dict:
    key_list = jax.random.split(jax.random.key(seed), 7)
    return {
        "layer_input": bell_draw(key_list[0], (TRACES, LENGTH, D), 1.0, 6.0, ((0, 8), (1, 32))),
        "projection": bell_draw(key_list[1], (D, 2 * N), D ** -0.5, 0.09375),
        "ssm_input": bell_draw(key_list[2], (TRACES, LENGTH, HP), 1.0, 6.0, ((0, 8), (1, 32))),
        "step_logit": bell_draw(key_list[3], (TRACES, LENGTH, H), 1.0, 4.0, ((0, 8), (1, 32)), jnp.float32),
        "decay_rate": jnp.clip(jnp.exp(jax.random.uniform(key_list[4], (H,), jnp.float32, math.log(0.00012207031), math.log(0.1))), 0.00012207031, 0.1),
        "output_grad": bell_draw(key_list[5], (TRACES, LENGTH, HP), 1.0, 6.0, ((0, 8), (1, 32))),
    }


def span_forward(ssm_block, b_block, c_block, logit_block, decay_rate, carry_in):
    row_count = ssm_block.shape[0]
    head_count = logit_block.shape[1]
    values = ssm_block.astype(jnp.float32).reshape(row_count, head_count, -1)
    b_vals = b_block.astype(jnp.float32)
    c_vals = c_block.astype(jnp.float32)
    dt_soft = jax.nn.softplus(logit_block)
    log_decay = jnp.cumsum(-decay_rate[None, :] * dt_soft, axis=0)
    causal = (lax.broadcasted_iota(jnp.int32, (row_count, row_count), 0) >= lax.broadcasted_iota(jnp.int32, (row_count, row_count), 1))[None, :, :]
    decay_heads = log_decay.T
    gap_log = decay_heads[:, :, None] - decay_heads[:, None, :]
    decays = jnp.exp(jnp.where(causal, gap_log, -jnp.inf))
    scores = jnp.einsum('tn,sn->ts', c_vals, b_vals, precision=lax.Precision.HIGHEST)
    weights = decays * scores[None, :, :] * dt_soft.T[:, None, :]
    inner = jnp.einsum('hts,shp->thp', weights, values, precision=lax.Precision.HIGHEST)
    outer = jnp.exp(log_decay)[:, :, None] * jnp.einsum('tn,hpn->thp', c_vals, carry_in, precision=lax.Precision.HIGHEST)
    to_end = jnp.exp(log_decay[-1][None, :] - log_decay) * dt_soft
    carry_out = jnp.exp(log_decay[-1])[:, None, None] * carry_in + jnp.einsum('sh,shp,sn->hpn', to_end, values, b_vals, precision=lax.Precision.HIGHEST)
    return (inner + outer, carry_out)

def reference(layer_input, projection, ssm_input, step_logit, decay_rate, output_grad):
    state_size = projection.shape[1] // 2

    def one_trace(items):
        tokens, x_rows, logit_rows, grad_rows = items
        projected = jnp.dot(tokens, projection, preferred_element_type=jnp.float32).astype(jnp.bfloat16)

        def forward(x_all, b_all, c_all, logit_all, rate_vec):
            blocks = (x_all.reshape(-1, L_DEV, x_all.shape[1]), b_all.reshape(-1, L_DEV, state_size), c_all.reshape(-1, L_DEV, state_size), logit_all.reshape(-1, L_DEV, logit_all.shape[1]))

            def advance(carry, block):
                result, carry_next = span_forward(block[0], block[1], block[2], block[3], rate_vec, carry)
                return (carry_next, result)
            start = jnp.zeros((H, P_SIZE, state_size), jnp.float32)
            unused, outputs = lax.scan(jax.checkpoint(advance), start, blocks)
            return outputs
        unused, pullback = jax.vjp(forward, x_rows, projected[:, :state_size], projected[:, state_size:], logit_rows, decay_rate)
        grad_x, grad_b, grad_c, grad_logit, grad_rate = pullback(grad_rows.astype(jnp.float32).reshape(-1, L_DEV, H, P_SIZE))
        grad_bc = jnp.concatenate([grad_b, grad_c], axis=1)
        grad_w = lax.dot_general(tokens, grad_bc, (((0,), (0,)), ((), ())), preferred_element_type=jnp.float32)
        return (grad_x, grad_logit, grad_rate, grad_w)
    grad_x, grad_logit, grad_rate, grad_w = lax.map(one_trace, (layer_input, ssm_input, step_logit, output_grad))
    return (grad_x, grad_logit, lax.optimization_barrier(jnp.sum(grad_rate, axis=0)), lax.optimization_barrier(jnp.sum(grad_w, axis=0)))
```

```python
import jax
import jax.numpy as jnp
from jax import lax
from jax.experimental import pallas as pl
from jax.experimental.pallas import tpu as pltpu
from jax.sharding import Mesh
from jax.sharding import PartitionSpec as P

ROWS = 128
HEADS = 64
HALF = 32
PAIRS = 16
TILE = PAIRS * 128
GROUP = 8
GROUPS = HEADS // GROUP
BF = jnp.bfloat16
F32 = jnp.float32
NN = (((1,), (0,)), ((), ()))
NT = (((1,), (1,)), ((), ()))
TN = (((0,), (0,)), ((), ()))
HIGH = lax.Precision.HIGHEST
VMEM = pl.BlockSpec(memory_space=pltpu.VMEM)
SMEM = pl.BlockSpec(memory_space=pltpu.SMEM)
SEQ = ("blk", "par")


def iota(shape, dim):
    return lax.broadcasted_iota(jnp.int32, shape, dim)


def dot(a, b, dims=NN):
    return lax.dot_general(a, b, dims, preferred_element_type=F32)


def dot_exact(a, b):
    return lax.dot_general(a, b, NN, precision=HIGH, preferred_element_type=F32)


def dot_split(a, b):
    head = a.astype(BF)
    tail = (a - head.astype(F32)).astype(BF)
    return dot(head, b) + dot(tail, b)


def spread(cols, pair, left):
    one = cols[:, 2 * pair : 2 * pair + 1]
    two = cols[:, 2 * pair + 1 : 2 * pair + 2]
    return jnp.where(left, one, two)


def turned(values, odd):
    other = jnp.concatenate([values[:, HALF:], values[:, :HALF]], axis=1)
    return jnp.where(odd == 0, values, other)


def lanes(pair, odd):
    half, place = divmod(pair, PAIRS)
    start = (odd if half == 0 else 1 - odd) * TILE + 128 * place
    return pl.ds(pl.multiple_of(start, 128), 128)


def call(kernel, outs, flops, moved, **more):
    return pl.pallas_call(
        kernel,
        out_shape=outs,
        compiler_params=pltpu.CompilerParams(vmem_limit_bytes=48 << 20),
        cost_estimate=pl.CostEstimate(flops=flops, bytes_accessed=moved, transcendentals=0),
        **more,
    )


def shape(*dims, dtype=F32):
    return jax.ShapeDtypeStruct(dims, dtype)


def turn_kernel(tok, out):
    for i in range(32):
        part = tok[:, 128 * i : 128 * i + 128].astype(F32).T
        for d in range(8):
            out[d, i] = part[16 * d : 16 * d + 16, :]


def project_kernel(
    odd_ref, tok, proj, x, logit, rate, bc_ref, c_ref, dt_ref, cg_ref, dtg_ref, ct_ref, rows_ref, keep, send
):
    odd = odd_ref[0]
    bc = dot(tok[...], proj[...]).astype(BF)
    bc_ref[...] = bc
    z = turned(logit[...], odd)
    dt = jnp.maximum(z, 0.0) + jnp.log1p(jnp.exp(-jnp.abs(z)))
    a = -turned(rate[...], odd) * dt
    lower = (iota((ROWS, ROWS), 0) >= iota((ROWS, ROWS), 1)).astype(F32)
    c = dot_exact(lower, a)
    c_ref[...] = c
    dt_ref[...] = dt
    ct_ref[...] = c.T
    for group in range(GROUPS):
        cg_ref[group] = c[:, GROUP * group : GROUP * group + GROUP]
        dtg_ref[group] = dt[:, GROUP * group : GROUP * group + GROUP]
    last = c[ROWS - 1 : ROWS, :]
    to_end = jnp.exp(last - c) * dt
    b_t = bc[:, :128].astype(F32).T.astype(BF)
    left = iota((ROWS, 128), 1) < 64
    left1 = iota((1, 128), 1) < 64
    for half, out in ((1, send), (0, keep)):
        for place in range(PAIRS):
            pair = half * PAIRS + place
            xw = x[:, lanes(pair, odd)].astype(F32) * spread(to_end, pair, left)
            out[128 * place : 128 * place + 128, :] = dot(b_t, xw.astype(BF))
            rows_ref[pair : pair + 1, :] = spread(last, pair, left1)
    send[TILE : TILE + PAIRS, :] = rows_ref[PAIRS : 2 * PAIRS, :]


def adjoint_kernel(odd_ref, bc, c_ref, rows, g, keep, send):
    odd = odd_ref[0]
    ec = jnp.exp(c_ref[...])
    c_t = bc[:, 128:].astype(F32).T.astype(BF)
    left = iota((ROWS, 128), 1) < 64
    for half, out in ((1, send), (0, keep)):
        for place in range(PAIRS):
            pair = half * PAIRS + place
            gw = g[:, lanes(pair, odd)].astype(F32) * spread(ec, pair, left)
            out[128 * place : 128 * place + 128, :] = dot(c_t, gw.astype(BF))
    send[TILE : TILE + PAIRS, :] = rows[PAIRS : 2 * PAIRS, :]


def intra_kernel(odd_ref, bc, cg, dtg, ct, x, g, u_ref, t_ref, s_ref, ds_ref):
    @pl.when(pl.program_id(0) == 0)
    def _():
        ds_ref[...] = jnp.zeros_like(ds_ref)

    sc_t = dot(bc[:, :128], bc[:, 128:], NT)
    causal = iota((ROWS, ROWS), 0) <= iota((ROWS, ROWS), 1)
    left = iota((ROWS, 128), 1) < 64
    ones = (left.astype(F32).astype(BF), (1.0 - left.astype(F32)).astype(BF))
    lane8 = iota((ROWS, GROUP), 1)
    s_all = jnp.zeros((ROWS, GROUP), F32)
    total = ds_ref[...]
    for pair in range(GROUP // 2):
        xs = x[:, 128 * pair : 128 * pair + 128]
        gs = g[:, 128 * pair : 128 * pair + 128]
        parts = []
        for side in range(2):
            h = 2 * pair + side
            gx = dot(xs * ones[side], gs, NT)
            gap = ct[h : h + 1, :] - cg[0, :, h : h + 1]
            decay = jnp.exp(jnp.where(causal, gap, -jnp.inf))
            parts.append(dot((decay * sc_t).astype(BF), gs))
            p = decay * gx * dtg[0, :, h : h + 1]
            total = total + p
            m = p * sc_t
            t_ref[h : h + 1, :] = jnp.sum(m, axis=0, keepdims=True)
            s_all = jnp.where(lane8 == h, jnp.sum(m, axis=1, keepdims=True), s_all)
        u_ref[:, 128 * pair : 128 * pair + 128] = jnp.where(left, parts[0], parts[1])
    s_ref[0] = s_all
    ds_ref[...] = total


def combine_kernel(rows, keep_s, keep_a, got_s, got_a, msg):
    for place in range(PAIRS):
        at = pl.ds(128 * place, 128)
        own = rows[place : place + 1, :]
        decay = jnp.exp(own)
        msg[place, 0:128, :] = decay * got_s[at, :] + keep_s[at, :]
        msg[place, 128:256, :] = decay * got_a[at, :] + keep_a[at, :]
        msg[place, 256:257, :] = own + got_s[TILE + place : TILE + place + 1, :]
        msg[place, 257:258, :] = own + got_a[TILE + place : TILE + place + 1, :]
        msg[place, 258:264, :] = jnp.zeros((6, 128), F32)


def scan_kernel(msg, out):
    state = jnp.zeros((128, 128), F32)
    for i in range(PAIRS):
        out[i, 0:128, :] = state
        state = jnp.exp(msg[i, 256:257, :]) * state + msg[i, 0:128, :]
    state = jnp.zeros((128, 128), F32)
    for i in range(PAIRS - 1, -1, -1):
        out[i, 128:256, :] = state
        state = jnp.exp(msg[i, 257:258, :]) * state + msg[i, 128:256, :]


def unfold_kernel(rows, keep_s, keep_a, got_s, got_a, back, s_own, a_own, s_next, a_next):
    for place in range(PAIRS):
        at = pl.ds(128 * place, 128)
        decay = jnp.exp(rows[place : place + 1, :])
        near_s = jnp.exp(got_s[TILE + place : TILE + place + 1, :])
        near_a = jnp.exp(got_a[TILE + place : TILE + place + 1, :])
        state = near_s * back[place, 0:128, :] + got_s[at, :]
        s_own[at, :] = state
        s_next[at, :] = decay * state + keep_s[at, :]
        adj = near_a * back[place, 128:256, :] + got_a[at, :]
        a_own[at, :] = adj
        a_next[at, :] = decay * adj + keep_a[at, :]


def outer_terms(half, odd, s_in, a_in, x, g, u, c_ref, dt_ref, bc, dots, store):
    cols = slice(HALF * half, HALF * half + HALF)
    c = c_ref[:, cols]
    dt = dt_ref[:, cols]
    last = c[ROWS - 1 : ROWS, :]
    end = jnp.exp(last - c)
    ec = jnp.exp(c)
    b_bf, c_bf = bc[:, :128], bc[:, 128:]
    left = iota((ROWS, 128), 1) < 64
    choice = iota((ROWS, HALF), 1) - (iota((ROWS, HALF), 0) >= 64).astype(jnp.int32)
    role = jnp.zeros((ROWS, HALF), F32)
    outer = jnp.zeros((ROWS, HALF), F32)
    grad_b = jnp.zeros((ROWS, 128), F32)
    grad_c = jnp.zeros((ROWS, 128), F32)
    for place in range(PAIRS):
        at = lanes(half * PAIRS + place, odd)
        rows = pl.ds(128 * place, 128)
        picked = (choice == 2 * place).astype(F32).astype(BF)
        state = s_in[rows, :]
        adj = a_in[rows, :]
        dots[place : place + 1, :] = jnp.sum(adj * state, axis=0, keepdims=True)
        adj = adj.astype(BF)
        state = state.astype(BF)
        gw = g[:, at].astype(F32) * spread(ec, place, left)
        role = role + dot_split(gw * dot(c_bf, state), picked)
        grad_c = grad_c + dot(gw.astype(BF), state, NT)
        wide = spread(end, place, left)
        wide_dt = spread(dt, place, left)
        add = dot(b_bf, adj) * wide
        xs = x[:, at].astype(F32)
        store(place, ((u[:, at] + add) * wide_dt).astype(BF))
        outer = outer + dot_split(xs * add, picked)
        grad_b = grad_b + dot((xs * (wide * wide_dt)).astype(BF), adj, NT)
    row, col = iota((128, HALF), 0), iota((128, HALF), 1)
    side = ((row >= 64).astype(jnp.int32) == col % 2).astype(F32)
    both = dot_exact(dots[...], side)
    mine = iota((PAIRS, HALF), 0) == iota((PAIRS, HALF), 1) // 2
    meet = jnp.exp(last) * jnp.sum(jnp.where(mine, both, 0.0), axis=0, keepdims=True)
    return role, outer, meet, grad_b, grad_c


def outer_kernel(
    odd_ref, s_in, a_in, x, g, u, c_ref, dt_ref, bc, ds, gx_ref, role_ref, outer_ref, meet_ref, gb_ref, gc_ref, dots
):
    def store(place, value):
        gx_ref[:, 128 * place : 128 * place + 128] = value

    role, outer, meet, grad_b, grad_c = outer_terms(
        0, odd_ref[0], s_in, a_in, x, g, u, c_ref, dt_ref, bc, dots, store
    )
    role_ref[...] = role
    outer_ref[...] = outer
    meet_ref[...] = jnp.broadcast_to(meet, (8, HALF))
    inner = ds[...].astype(BF)
    gb_ref[...] = grad_b + dot(inner, bc[:, 128:])
    gc_ref[...] = grad_c + dot(inner, bc[:, :128], TN)


def finish_kernel(
    odd_ref, s_in, a_in, x, g, u, c_ref, dt_ref, bc, gx_own, role_own, outer_own, meet_own, gb_own, gc_own,
    t_rows, s_cols, logit, rate, gx_ref, step_ref, msg, dots,
):
    odd = odd_ref[0]

    def store(place, value):
        gx_ref[:, lanes(PAIRS + place, odd)] = value

    role, outer, meet, grad_b, grad_c = outer_terms(
        1, odd, s_in, a_in, x, g, u, c_ref, dt_ref, bc, dots, store
    )
    for place in range(PAIRS):
        gx_ref[:, lanes(place, odd)] = gx_own[:, 128 * place : 128 * place + 128]
    msg[0:128, 0:128] = (gb_own[...] + grad_b).astype(BF).astype(F32)
    msg[0:128, 128:256] = (gc_own[...] + grad_c).astype(BF).astype(F32)
    dt = dt_ref[...]
    role_t = jnp.concatenate([role_own[...], role], axis=1) + t_rows[...].T
    outer = jnp.concatenate([outer_own[...], outer], axis=1)
    meet = jnp.concatenate([meet_own[0:1, :], meet], axis=1)
    role_s = jnp.concatenate([s_cols[k] for k in range(GROUPS)], axis=1)
    row, col = iota((ROWS, ROWS), 0), iota((ROWS, ROWS), 1)
    later = (col >= row).astype(F32)
    before = (col < row).astype(F32)
    da = dot_exact(later, role_t - role_s) + dot_exact(before, outer * dt) + meet
    ddt = turned(role_s / dt + outer, odd) - rate[...] * turned(da, odd)
    step_ref[...] = ddt / (1.0 + jnp.exp(-logit[...]))
    rate_row = turned(-jnp.sum(dt * da, axis=0, keepdims=True), odd)
    wide = jnp.concatenate([rate_row, jnp.zeros((1, 256 - HEADS), F32)], axis=1)
    msg[128:136, :] = jnp.broadcast_to(wide, (8, 256))


def weight_kernel(tok, got, msg):
    total = jnp.zeros((512, 256), F32)
    rates = jnp.zeros((8, 256), F32)
    for d in range(8):
        total = total + dot(tok[d].astype(BF), got[d, 0:128, :].astype(BF))
        rates = rates + got[d, 128:136, :]
    for i in range(32):
        msg[i, 0:16, :] = total[16 * i : 16 * i + 16, :]
        msg[i, 16:24, :] = rates


def shards(layer_input, projection, ssm_input, step_logit, decay_rate, output_grad):
    tok, x, g, logit = layer_input[0], ssm_input[0], output_grad[0], step_logit[0]
    rate = decay_rate[None, :]
    width = x.shape[1]
    odd = lax.axis_index("par").astype(jnp.int32)[None]
    up = [(i, i + 1) for i in range(31)]
    down = [(i + 1, i) for i in range(31)]

    bc, c, dt, cg, dtg, ct, rows, keep_s, send_s = call(
        project_kernel,
        (
            shape(ROWS, 256, dtype=BF),
            shape(ROWS, HEADS),
            shape(ROWS, HEADS),
            shape(GROUPS, ROWS, GROUP),
            shape(GROUPS, ROWS, GROUP),
            shape(HEADS, ROWS),
            shape(2 * PAIRS, 128),
            shape(TILE, 128),
            shape(TILE + PAIRS, 128),
        ),
        400_000_000,
        6 << 20,
        in_specs=[SMEM] + [VMEM] * 5,
        out_specs=(VMEM,) * 9,
        name="project",
    )(odd, tok, projection, x, logit, rate)
    got_s = lax.ppermute(send_s, SEQ, up)
    keep_a, send_a = call(
        adjoint_kernel,
        (shape(TILE, 128), shape(TILE + PAIRS, 128)),
        140_000_000,
        3 << 20,
        in_specs=[SMEM] + [VMEM] * 4,
        out_specs=(VMEM,) * 2,
        name="adjoint",
    )(odd, bc, c, rows, g)
    got_a = lax.ppermute(send_a, SEQ, down)

    turned_tok = call(
        turn_kernel,
        shape(8, 32, 16, 128),
        1_000_000,
        3 << 20,
        in_specs=[VMEM],
        out_specs=VMEM,
        name="turn",
    )(tok)
    all_tok = lax.all_to_all(turned_tok, "dp", 0, 0).reshape(8, 512, 128)

    wide = GROUP * 64

    def place(i, odd):
        return (i + odd[0] * (GROUPS // 2)) % GROUPS

    u, t_rows, s_cols, ds = call(
        intra_kernel,
        (
            shape(ROWS, width),
            shape(HEADS, ROWS),
            shape(GROUPS, ROWS, GROUP),
            shape(ROWS, ROWS),
        ),
        800_000_000,
        20 << 20,
        grid_spec=pltpu.PrefetchScalarGridSpec(
            num_scalar_prefetch=1,
            grid=(GROUPS,),
            in_specs=[
                pl.BlockSpec((ROWS, 256), lambda i, odd: (0, 0)),
                pl.BlockSpec((1, ROWS, GROUP), lambda i, odd: (i, 0, 0)),
                pl.BlockSpec((1, ROWS, GROUP), lambda i, odd: (i, 0, 0)),
                pl.BlockSpec((GROUP, ROWS), lambda i, odd: (i, 0)),
                pl.BlockSpec((ROWS, wide), lambda i, odd: (0, place(i, odd))),
                pl.BlockSpec((ROWS, wide), lambda i, odd: (0, place(i, odd))),
            ],
            out_specs=(
                pl.BlockSpec((ROWS, wide), lambda i, odd: (0, place(i, odd))),
                pl.BlockSpec((GROUP, ROWS), lambda i, odd: (i, 0)),
                pl.BlockSpec((1, ROWS, GROUP), lambda i, odd: (i, 0, 0)),
                pl.BlockSpec((ROWS, ROWS), lambda i, odd: (0, 0)),
            ),
        ),
        name="intra",
    )(odd, bc, cg, dtg, ct, x, g)

    sent = call(
        combine_kernel,
        shape(PAIRS, 264, 128),
        4_000_000,
        6 << 20,
        in_specs=[VMEM] * 5,
        out_specs=VMEM,
        name="combine",
    )(rows, keep_s, keep_a, got_s, got_a)
    held = lax.all_to_all(sent, "blk", 0, 0)
    scanned = call(
        scan_kernel,
        shape(PAIRS, 256, 128),
        4_000_000,
        4 << 20,
        in_specs=[VMEM],
        out_specs=VMEM,
        name="scan",
    )(held)
    back = lax.all_to_all(scanned, "blk", 0, 0)
    s_own, a_own, s_next, a_next = call(
        unfold_kernel,
        (shape(TILE, 128),) * 4,
        8_000_000,
        10 << 20,
        in_specs=[VMEM] * 6,
        out_specs=(VMEM,) * 4,
        name="unfold",
    )(rows, keep_s, keep_a, got_s, got_a, back)
    s_far = lax.ppermute(s_next, SEQ, up)
    a_far = lax.ppermute(a_next, SEQ, down)

    gx_own, *own = call(
        outer_kernel,
        (
            shape(ROWS, TILE, dtype=BF),
            shape(ROWS, HALF),
            shape(ROWS, HALF),
            shape(8, HALF),
            shape(ROWS, 128),
            shape(ROWS, 128),
        ),
        500_000_000,
        6 << 20,
        in_specs=[SMEM] + [VMEM] * 9,
        out_specs=(VMEM,) * 6,
        scratch_shapes=[pltpu.VMEM((PAIRS, 128), F32)],
        name="outer",
    )(odd, s_own, a_own, x, g, u, c, dt, bc, ds)
    gx, step_grad, part = call(
        finish_kernel,
        (shape(ROWS, width, dtype=BF), shape(ROWS, HEADS), shape(136, 256)),
        500_000_000,
        6 << 20,
        in_specs=[SMEM] + [VMEM] * 18,
        out_specs=(VMEM,) * 3,
        scratch_shapes=[pltpu.VMEM((PAIRS, 128), F32)],
        name="finish",
    )(odd, s_far, a_far, x, g, u, c, dt, bc, gx_own, *own, t_rows, s_cols, logit, rate)

    parts = lax.all_to_all(jnp.broadcast_to(part[None], (8, 136, 256)), "dp", 0, 0)
    weight = call(
        weight_kernel,
        shape(32, 24, 256),
        300_000_000,
        4 << 20,
        in_specs=[VMEM] * 2,
        out_specs=VMEM,
        name="weight",
    )(all_tok, parts)
    summed = jnp.sum(lax.all_to_all(weight, SEQ, 0, 0), axis=0)
    full = lax.all_gather(summed[:16], "dp", tiled=True)
    return gx[None], step_grad[None], summed[16, :HEADS], full


def solution(mesh):
    devices = mesh.devices.reshape(16, 2, 8)
    parts = Mesh(devices, ("blk", "par", "dp"))
    placed = (
        P("dp", SEQ, None),
        P(),
        P("dp", SEQ, None),
        P("dp", SEQ, None),
        P(),
        P("dp", SEQ, None),
    )
    return jax.shard_map(
        shards,
        mesh=parts,
        in_specs=placed,
        out_specs=(P("dp", SEQ, None), P("dp", SEQ, None), P(), P(SEQ, None)),
        check_vma=False,
    )
```

```python
import functools

import jax
import jax.numpy as jnp
from jax import lax
from jax.experimental import pallas as pl
from jax.experimental.pallas import tpu as pltpu
from jax.sharding import Mesh
from jax.sharding import PartitionSpec as P

ROWS = 128
HEADS = 64
SLOTS = 4
PART = HEADS // SLOTS
PAIRS = PART // 2
ALL_PAIRS = HEADS // 2
TILE = PAIRS * 128
MIRROR = (2, 1, 0, 3)
GROUP = 8
GROUPS = HEADS // GROUP
BF = jnp.bfloat16
F32 = jnp.float32
NN = (((1,), (0,)), ((), ()))
NT = (((1,), (1,)), ((), ()))
TN = (((0,), (0,)), ((), ()))
HIGH = lax.Precision.HIGHEST
VMEM = pl.BlockSpec(memory_space=pltpu.VMEM)
SMEM = pl.BlockSpec(memory_space=pltpu.SMEM)
HBM = pl.BlockSpec(memory_space=pltpu.HBM)
SEQ = ("x", "quad", "turn")
BLOCK = ("x", "quad")
CHUNKS = 4
CHUNK = 1024


def iota(shape, dim):
    return lax.broadcasted_iota(jnp.int32, shape, dim)


def dot(a, b, dims=NN):
    return lax.dot_general(a, b, dims, preferred_element_type=F32)


def dot_exact(a, b):
    return lax.dot_general(a, b, NN, precision=HIGH, preferred_element_type=F32)


def dot_split(a, b):
    head = a.astype(BF)
    tail = (a - head.astype(F32)).astype(BF)
    return dot(head, b) + dot(tail, b)


def spread(cols, pair, left):
    one = cols[:, 2 * pair : 2 * pair + 1]
    two = cols[:, 2 * pair + 1 : 2 * pair + 2]
    return jnp.where(left, one, two)


def turned(values, turn):
    parts = [values[:, PART * k : PART * k + PART] for k in range(SLOTS)]
    out = values
    for t in range(SLOTS):
        order = jnp.concatenate([parts[(t + 3 - k) % SLOTS] for k in range(SLOTS)], axis=1)
        out = jnp.where(turn == t, order, out)
    return out


def lanes(pair, turn):
    slot, place = divmod(pair, PAIRS)
    start = lax.rem(turn + 3 - slot, SLOTS) * TILE + 128 * place
    return pl.ds(pl.multiple_of(start, 128), 128)


def tile(place):
    return slice(128 * place, 128 * place + 128)


def call(kernel, outs, flops, moved, room=8, **more):
    return pl.pallas_call(
        kernel,
        out_shape=outs,
        compiler_params=pltpu.CompilerParams(vmem_limit_bytes=room << 20),
        cost_estimate=pl.CostEstimate(flops=flops, bytes_accessed=moved, transcendentals=0),
        **more,
    )


def shape(*dims, dtype=F32):
    return jax.ShapeDtypeStruct(dims, dtype)


def advance(name, kernel, *fixed):
    return call(
        functools.partial(kernel, *fixed),
        shape(TILE + PAIRS if kernel is gather_step_kernel else TILE, 128),
        1_000_000,
        2 << 20,
        in_specs=[VMEM] * 3,
        out_specs=VMEM,
        name=name,
    )


def turn_kernel(tok, out):
    for i in range(32):
        at = slice(128 * i, 128 * i + 128)
        out[at, :] = tok[:, at].astype(F32).T.astype(BF)


def project_kernel(
    turn_ref, logit, rate, tok_hbm, proj_hbm, x_hbm, bc_ref, c_ref, dt_ref, rows_ref, xw_ref, send, tok, proj, x, sems
):
    copies = []
    for k in range(CHUNKS):
        at = pl.ds(k * CHUNK, CHUNK)
        copies.append(
            (
                pltpu.make_async_copy(tok_hbm.at[:, at], tok.at[:, at], sems.at[0, k]),
                pltpu.make_async_copy(proj_hbm.at[at, :], proj.at[at, :], sems.at[1, k]),
            )
        )
        for copy in copies[-1]:
            copy.start()
    fetch_x = pltpu.make_async_copy(x_hbm, x, sems.at[2, 0])
    fetch_x.start()
    turn = turn_ref[0]
    z = turned(logit[...].T, turn)
    dt = jnp.maximum(z, 0.0) + jnp.log1p(jnp.exp(-jnp.abs(z)))
    a = -turned(rate[...], turn) * dt
    lower = (iota((ROWS, ROWS), 0) >= iota((ROWS, ROWS), 1)).astype(F32)
    c = dot_exact(lower, a)
    c_ref[...] = c
    dt_ref[...] = dt
    last = c[ROWS - 1 : ROWS, :]
    to_end = jnp.exp(last - c) * dt
    left = iota((ROWS, 128), 1) < 64
    left1 = iota((1, 128), 1) < 64
    for pair in range(ALL_PAIRS):
        rows_ref[pair : pair + 1, :] = spread(last, pair, left1)
    send[TILE : TILE + PAIRS, :] = rows_ref[0:PAIRS, :]
    total = jnp.zeros((ROWS, 256), F32)
    for k in range(CHUNKS):
        for copy in copies[k]:
            copy.wait()
        at = slice(k * CHUNK, k * CHUNK + CHUNK)
        total = total + dot(tok[:, at], proj[at, :])
    bc = total.astype(BF)
    bc_ref[...] = bc
    b_t = bc[:, :128].astype(F32).T.astype(BF)
    fetch_x.wait()
    for pair in range(ALL_PAIRS):
        at = lanes(pair, turn)
        xw = (x[:, at].astype(F32) * spread(to_end, pair, left)).astype(BF)
        xw_ref[:, at] = xw
        if pair < PAIRS:
            send[tile(pair), :] = dot(b_t, xw)


def adjoint_kernel(turn_ref, bc, c_ref, rows, g, gw_ref, send):
    turn = turn_ref[0]
    ec = jnp.exp(c_ref[...])
    c_t = bc[:, 128:].astype(F32).T.astype(BF)
    left = iota((ROWS, 128), 1) < 64
    first = MIRROR[0] * PAIRS
    for pair in range(ALL_PAIRS):
        at = lanes(pair, turn)
        gw = (g[:, at].astype(F32) * spread(ec, pair, left)).astype(BF)
        gw_ref[:, at] = gw
        if first <= pair < first + PAIRS:
            send[tile(pair - first), :] = dot(c_t, gw)
    send[TILE : TILE + PAIRS, :] = rows[first : first + PAIRS, :]


def rest_kernel(turn_ref, bc, c_ref, dt_ref, xw, gw, rest_s, rest_a, cg_ref, dtg_ref, ct_ref):
    turn = turn_ref[0]
    both = bc[...].astype(F32)
    b_t = both[:, :128].T.astype(BF)
    c_t = both[:, 128:].T.astype(BF)
    for k in range(1, SLOTS):
        for place in range(PAIRS):
            rest_s[k - 1, tile(place), :] = dot(b_t, xw[:, lanes(k * PAIRS + place, turn)])
            rest_a[k - 1, tile(place), :] = dot(c_t, gw[:, lanes(MIRROR[k] * PAIRS + place, turn)])
    c = c_ref[...]
    ct_ref[...] = c.T
    for group in range(GROUPS):
        cg_ref[group] = c[:, GROUP * group : GROUP * group + GROUP]
        dtg_ref[group] = dt_ref[:, GROUP * group : GROUP * group + GROUP]


def gather_step_kernel(slot, k, rows, got, rest, out):
    for place in range(PAIRS):
        own = rows[slot * PAIRS + place : slot * PAIRS + place + 1, :]
        out[tile(place), :] = jnp.exp(own) * got[tile(place), :] + rest[k - 1, tile(place), :]
    out[TILE : TILE + PAIRS, :] = got[TILE : TILE + PAIRS, :] + rows[slot * PAIRS : slot * PAIRS + PAIRS, :]


def spread_step_kernel(slot, rows, state, local, out):
    for place in range(PAIRS):
        own = rows[slot * PAIRS + place : slot * PAIRS + place + 1, :]
        out[tile(place), :] = jnp.exp(own) * state[tile(place), :] + local[tile(place), :]


def spread_rest_kernel(slot, rows, state, rest, out):
    spread_step_kernel(slot, rows, state, rest.at[0], out)


def intra_kernel(turn_ref, bc, cg, dtg, ct, x, g, u_ref, t_ref, s_ref, ds_ref):
    @pl.when(pl.program_id(0) == 0)
    def _():
        ds_ref[...] = jnp.zeros_like(ds_ref)

    sc_t = dot(bc[:, :128], bc[:, 128:], NT)
    causal = iota((ROWS, ROWS), 0) <= iota((ROWS, ROWS), 1)
    left = iota((ROWS, 128), 1) < 64
    ones = (left.astype(F32).astype(BF), (1.0 - left.astype(F32)).astype(BF))
    lane8 = iota((ROWS, GROUP), 1)
    s_all = jnp.zeros((ROWS, GROUP), F32)
    total = ds_ref[...]
    for pair in range(GROUP // 2):
        xs = x[:, 128 * pair : 128 * pair + 128]
        gs = g[:, 128 * pair : 128 * pair + 128]
        parts = []
        for side in range(2):
            h = 2 * pair + side
            gx = dot(xs * ones[side], gs, NT)
            gap = ct[h : h + 1, :] - cg[0, :, h : h + 1]
            decay = jnp.exp(jnp.where(causal, gap, -jnp.inf))
            parts.append(dot((decay * sc_t).astype(BF), gs))
            p = decay * gx * dtg[0, :, h : h + 1]
            total = total + p
            m = p * sc_t
            t_ref[h : h + 1, :] = jnp.sum(m, axis=0, keepdims=True)
            s_all = jnp.where(lane8 == h, jnp.sum(m, axis=1, keepdims=True), s_all)
        u_ref[:, 128 * pair : 128 * pair + 128] = jnp.where(left, parts[0], parts[1])
    s_ref[0] = s_all
    ds_ref[...] = total


def combine_kernel(rows, rest_s, rest_a, got_s, got_a, msg):
    for place in range(PAIRS):
        own = rows[3 * PAIRS + place : 3 * PAIRS + place + 1, :]
        decay = jnp.exp(own)
        msg[place, 0:128, :] = decay * got_s[tile(place), :] + rest_s[2, tile(place), :]
        msg[place, 128:256, :] = decay * got_a[tile(place), :] + rest_a[2, tile(place), :]
        msg[place, 256:257, :] = own + got_s[TILE + place : TILE + place + 1, :]
        msg[place, 257:258, :] = own + got_a[TILE + place : TILE + place + 1, :]
        msg[place, 258:264, :] = jnp.zeros((6, 128), F32)


def scan_kernel(msg, out):
    state = jnp.zeros((128, 128), F32)
    for i in range(PAIRS):
        out[i, 0:128, :] = state
        state = jnp.exp(msg[i, 256:257, :]) * state + msg[i, 0:128, :]
    state = jnp.zeros((128, 128), F32)
    for i in range(PAIRS - 1, -1, -1):
        out[i, 128:256, :] = state
        state = jnp.exp(msg[i, 257:258, :]) * state + msg[i, 128:256, :]


def near_states(got_s, got_a, back, place):
    mark = TILE + place
    state = jnp.exp(got_s[mark : mark + 1, :]) * back[place, 0:128, :] + got_s[tile(place), :]
    adj = jnp.exp(got_a[mark : mark + 1, :]) * back[place, 128:256, :] + got_a[tile(place), :]
    return state, adj


def unfold_kernel(rows, rest_s, rest_a, got_s, got_a, back, s_next, a_next):
    for place in range(PAIRS):
        state, adj = near_states(got_s, got_a, back, place)
        decay = jnp.exp(rows[3 * PAIRS + place : 3 * PAIRS + place + 1, :])
        s_next[tile(place), :] = decay * state + rest_s[2, tile(place), :]
        a_next[tile(place), :] = decay * adj + rest_a[2, tile(place), :]


def outer_terms(slot, turn, s_in, a_in, x, g, u, c_ref, dt_ref, bc, dots, store):
    cols = slice(PART * slot, PART * slot + PART)
    c = c_ref[:, cols]
    dt = dt_ref[:, cols]
    last = c[ROWS - 1 : ROWS, :]
    end = jnp.exp(last - c)
    ec = jnp.exp(c)
    b_bf, c_bf = bc[:, :128], bc[:, 128:]
    left = iota((ROWS, 128), 1) < 64
    choice = iota((ROWS, PART), 1) - (iota((ROWS, PART), 0) >= 64).astype(jnp.int32)
    role = jnp.zeros((ROWS, PART), F32)
    outer = jnp.zeros((ROWS, PART), F32)
    for place in range(PAIRS):
        at = lanes(slot * PAIRS + place, turn)
        picked = (choice == 2 * place).astype(F32).astype(BF)
        state = s_in[tile(place), :]
        adj = a_in[tile(place), :]
        dots[place : place + 1, :] = jnp.sum(adj * state, axis=0, keepdims=True)
        gw = g[:, at].astype(F32) * spread(ec, place, left)
        role = role + dot_split(gw * dot(c_bf, state.astype(BF)), picked)
        add = dot(b_bf, adj.astype(BF)) * spread(end, place, left)
        store(place, ((u[:, at] + add) * spread(dt, place, left)).astype(BF))
        outer = outer + dot_split(x[:, at].astype(F32) * add, picked)
    row, col = iota((128, PART), 0), iota((128, PART), 1)
    side = ((row >= 64).astype(jnp.int32) == col % 2).astype(F32)
    both = dot_exact(dots[...], side)
    mine = iota((PAIRS, PART), 0) == iota((PAIRS, PART), 1) // 2
    meet = jnp.exp(last) * jnp.sum(jnp.where(mine, both, 0.0), axis=0, keepdims=True)
    return role, outer, meet


def outer_kernel(
    slot, turn_ref, s_in, a_in, x, g, u, c_ref, dt_ref, bc, gx_ref, role_ref, outer_ref, meet_ref, dots
):
    def store(place, value):
        gx_ref[:, tile(place)] = value

    role, outer, meet = outer_terms(slot, turn_ref[0], s_in, a_in, x, g, u, c_ref, dt_ref, bc, dots, store)
    role_ref[...] = role
    outer_ref[...] = outer
    meet_ref[...] = jnp.broadcast_to(meet, (8, PART))


def near_kernel(turn_ref, got_s, got_a, back, xw, gw, bc, ds, out, s_own, a_own):
    turn = turn_ref[0]
    inner = ds[...].astype(BF)
    grad_b = dot(inner, bc[:, 128:])
    grad_c = dot(inner, bc[:, :128], TN)
    for place in range(PAIRS):
        at = lanes(3 * PAIRS + place, turn)
        state, adj = near_states(got_s, got_a, back, place)
        s_own[tile(place), :] = state
        a_own[tile(place), :] = adj
        grad_b = grad_b + dot(xw[:, at], adj.astype(BF), NT)
        grad_c = grad_c + dot(gw[:, at], state.astype(BF), NT)
    out[:, :128] = grad_b
    out[:, 128:] = grad_c


def more_terms(turn, k, s_in, a_in, xw, gw, grad_b, grad_c):
    for place in range(PAIRS):
        grad_b = grad_b + dot(xw[:, lanes(MIRROR[k] * PAIRS + place, turn)], a_in[tile(place), :].astype(BF), NT)
        grad_c = grad_c + dot(gw[:, lanes(k * PAIRS + place, turn)], s_in[tile(place), :].astype(BF), NT)
    return grad_b, grad_c


def middle_kernel(turn_ref, s_0, a_0, s_1, a_1, xw, gw, near, out):
    turn = turn_ref[0]
    grads = near[:, :128], near[:, 128:]
    grads = more_terms(turn, 0, s_0, a_0, xw, gw, *grads)
    grads = more_terms(turn, 1, s_1, a_1, xw, gw, *grads)
    out[:, :128] = grads[0]
    out[:, 128:] = grads[1]


def far_kernel(turn_ref, core_ref, s_in, a_in, xw, gw, near, tok_t, keep, send):
    first = core_ref[0] == 0
    grad_b, grad_c = more_terms(turn_ref[0], 2, s_in, a_in, xw, gw, near[:, :128], near[:, 128:])
    both = jnp.concatenate([grad_b.astype(BF), grad_c.astype(BF)], axis=1)
    for i in range(32):
        part = dot(tok_t[128 * i : 128 * i + 128, :], both)
        x, z = divmod(i, 8)
        rows = slice(16 * z, 16 * z + 16)
        for y in range(4):
            one = part[32 * y : 32 * y + 16, :]
            two = part[32 * y + 16 : 32 * y + 32, :]
            keep[4 * x + y, rows, :] = jnp.where(first, one, two)
            send[4 * x + y, rows, :] = jnp.where(first, two, one)


def join_kernel(keep, got, rates, msg):
    for k in range(16):
        msg[k, 0:128, :] = keep[k] + got[k]
        msg[k, 128:136, :] = rates[...]


def fold_kernel(msg, out):
    total = msg[0]
    for k in range(1, 16):
        total = total + msg[k]
    for z in range(8):
        out[z, 0:16, :] = total[16 * z : 16 * z + 16, :]
        out[z, 16:24, :] = total[128:136, :]


def last_kernel(msg, out):
    total = msg[0]
    for k in range(1, 8):
        total = total + msg[k]
    for k in range(8):
        out[k] = total


def finish_kernel(
    turn_ref, s_0, a_0, s_2, a_2, x, g, u, c_ref, dt_ref, bc, gx_1, role_1, outer_1, meet_1, gx_3, role_3, outer_3,
    meet_3, t_rows, s_cols, logit, rate, gx_ref, step_ref, rate_ref, dots,
):
    turn = turn_ref[0]

    def terms(slot, state, adj):
        def store(place, value):
            gx_ref[:, lanes(slot * PAIRS + place, turn)] = value

        return outer_terms(slot, turn, state, adj, x, g, u, c_ref, dt_ref, bc, dots, store)

    zero, two = terms(0, s_0, a_0), terms(2, s_2, a_2)
    for place in range(PAIRS):
        gx_ref[:, lanes(PAIRS + place, turn)] = gx_1[:, tile(place)]
        gx_ref[:, lanes(3 * PAIRS + place, turn)] = gx_3[:, tile(place)]
    dt = dt_ref[...]
    role_t = jnp.concatenate([zero[0], role_1[...], two[0], role_3[...]], axis=1) + t_rows[...].T
    outer = jnp.concatenate([zero[1], outer_1[...], two[1], outer_3[...]], axis=1)
    meet = jnp.concatenate([zero[2], meet_1[0:1, :], two[2], meet_3[0:1, :]], axis=1)
    role_s = jnp.concatenate([s_cols[k] for k in range(GROUPS)], axis=1)
    row, col = iota((ROWS, ROWS), 0), iota((ROWS, ROWS), 1)
    later = (col >= row).astype(F32)
    before = (col < row).astype(F32)
    da = dot_exact(later, role_t - role_s) + dot_exact(before, outer * dt) + meet
    ddt = turned(role_s / dt + outer, turn) - rate[...] * turned(da, turn)
    step_ref[...] = ddt.T / (1.0 + jnp.exp(-logit[...]))
    rate_row = turned(-jnp.sum(dt * da, axis=0, keepdims=True), turn)
    wide = jnp.concatenate([rate_row, jnp.zeros((1, 256 - HEADS), F32)], axis=1)
    rate_ref[...] = jnp.broadcast_to(wide, (8, 256))


def shards(layer_input, projection, ssm_input, step_logit, decay_rate, output_grad):
    tok, x, g, logit = layer_input[0], ssm_input[0], output_grad[0], step_logit[0].T
    rate = decay_rate[None, :]
    width = x.shape[1]
    turn = lax.axis_index("turn").astype(jnp.int32)[None]
    core = lax.axis_index("c").astype(jnp.int32)[None]
    up = [(i, i + 1) for i in range(31)]
    down = [(i + 1, i) for i in range(31)]

    bc, c, dt, rows, xw, send_s = call(
        project_kernel,
        (
            shape(ROWS, 256, dtype=BF),
            shape(ROWS, HEADS),
            shape(ROWS, HEADS),
            shape(ALL_PAIRS, 128),
            shape(ROWS, width, dtype=BF),
            shape(TILE + PAIRS, 128),
        ),
        400_000_000,
        6 << 20,
        room=52,
        in_specs=[SMEM, VMEM, VMEM, HBM, HBM, HBM],
        out_specs=(VMEM,) * 6,
        scratch_shapes=[
            pltpu.VMEM((ROWS, width), BF),
            pltpu.VMEM((width, 256), BF),
            pltpu.VMEM((ROWS, width), BF),
            pltpu.SemaphoreType.DMA((3, CHUNKS)),
        ],
        name="project",
    )(turn, logit, rate, tok, projection, x)
    got_s = lax.ppermute(send_s, SEQ, up)
    gw, send_a = call(
        adjoint_kernel,
        (shape(ROWS, width, dtype=BF), shape(TILE + PAIRS, 128)),
        140_000_000,
        3 << 20,
        in_specs=[SMEM] + [VMEM] * 4,
        out_specs=(VMEM,) * 2,
        name="adjoint",
    )(turn, bc, c, rows, g)
    got_a = lax.ppermute(send_a, SEQ, down)

    rest_s, rest_a, cg, dtg, ct = call(
        rest_kernel,
        (
            shape(3, TILE, 128),
            shape(3, TILE, 128),
            shape(GROUPS, ROWS, GROUP),
            shape(GROUPS, ROWS, GROUP),
            shape(HEADS, ROWS),
        ),
        200_000_000,
        6 << 20,
        in_specs=[SMEM] + [VMEM] * 5,
        out_specs=(VMEM,) * 5,
        name="rest",
    )(turn, bc, c, dt, xw, gw)
    tok_t = call(
        turn_kernel,
        shape(width, ROWS, dtype=BF),
        1_000_000,
        3 << 20,
        in_specs=[VMEM],
        out_specs=VMEM,
        name="turn",
    )(tok)

    wide = GROUP * 64

    def place(i, turn):
        return lax.rem(turn[0] + 3 - i // 2, SLOTS) * 2 + i % 2

    u, t_rows, s_cols, ds = call(
        intra_kernel,
        (
            shape(ROWS, width),
            shape(HEADS, ROWS),
            shape(GROUPS, ROWS, GROUP),
            shape(ROWS, ROWS),
        ),
        800_000_000,
        20 << 20,
        grid_spec=pltpu.PrefetchScalarGridSpec(
            num_scalar_prefetch=1,
            grid=(GROUPS,),
            in_specs=[
                pl.BlockSpec((ROWS, 256), lambda i, turn: (0, 0)),
                pl.BlockSpec((1, ROWS, GROUP), lambda i, turn: (i, 0, 0)),
                pl.BlockSpec((1, ROWS, GROUP), lambda i, turn: (i, 0, 0)),
                pl.BlockSpec((GROUP, ROWS), lambda i, turn: (i, 0)),
                pl.BlockSpec((ROWS, wide), lambda i, turn: (0, place(i, turn))),
                pl.BlockSpec((ROWS, wide), lambda i, turn: (0, place(i, turn))),
            ],
            out_specs=(
                pl.BlockSpec((ROWS, wide), lambda i, turn: (0, place(i, turn))),
                pl.BlockSpec((GROUP, ROWS), lambda i, turn: (i, 0)),
                pl.BlockSpec((1, ROWS, GROUP), lambda i, turn: (i, 0, 0)),
                pl.BlockSpec((ROWS, ROWS), lambda i, turn: (0, 0)),
            ),
        ),
        name="intra",
    )(turn, bc, cg, dtg, ct, x, g)
    for k in (1, 2):
        got_s = lax.ppermute(advance("gather_s", gather_step_kernel, k, k)(rows, got_s, rest_s), SEQ, up)
        got_a = lax.ppermute(advance("gather_a", gather_step_kernel, MIRROR[k], k)(rows, got_a, rest_a), SEQ, down)
    got_s, got_a, u, tok_t = lax.optimization_barrier((got_s, got_a, u, tok_t))

    sent = call(
        combine_kernel,
        shape(PAIRS, 264, 128),
        4_000_000,
        4 << 20,
        in_specs=[VMEM] * 5,
        out_specs=VMEM,
        name="combine",
    )(rows, rest_s, rest_a, got_s, got_a)
    held = lax.all_to_all(sent, BLOCK, 0, 0)
    scanned = call(
        scan_kernel,
        shape(PAIRS, 256, 128),
        4_000_000,
        4 << 20,
        in_specs=[VMEM],
        out_specs=VMEM,
        name="scan",
    )(held)
    back = lax.all_to_all(scanned, BLOCK, 0, 0)
    s_next, a_next = call(
        unfold_kernel,
        (shape(TILE, 128),) * 2,
        8_000_000,
        4 << 20,
        in_specs=[VMEM] * 6,
        out_specs=(VMEM,) * 2,
        name="unfold",
    )(rows, rest_s, rest_a, got_s, got_a, back)
    s_0 = lax.ppermute(s_next, SEQ, up)
    a_0 = lax.ppermute(a_next, SEQ, down)
    near, s_own, a_own = call(
        near_kernel,
        (shape(ROWS, 256), shape(TILE, 128), shape(TILE, 128)),
        140_000_000,
        4 << 20,
        in_specs=[SMEM] + [VMEM] * 7,
        out_specs=(VMEM,) * 3,
        name="near",
    )(turn, got_s, got_a, back, xw, gw, bc, ds)

    def outer_part(slot, state, adj):
        return call(
            functools.partial(outer_kernel, slot),
            (
                shape(ROWS, TILE, dtype=BF),
                shape(ROWS, PART),
                shape(ROWS, PART),
                shape(8, PART),
            ),
            250_000_000,
            6 << 20,
            in_specs=[SMEM] + [VMEM] * 8,
            out_specs=(VMEM,) * 4,
            scratch_shapes=[pltpu.VMEM((PAIRS, 128), F32)],
            name="outer",
        )(turn, state, adj, x, g, u, c, dt, bc)

    own = outer_part(3, s_own, a_own)
    s_1 = lax.ppermute(advance("spread_s", spread_step_kernel, 0)(rows, s_0, send_s), SEQ, up)
    a_1 = lax.ppermute(advance("spread_a", spread_step_kernel, MIRROR[0])(rows, a_0, send_a), SEQ, down)
    s_2 = lax.ppermute(advance("spread_s", spread_rest_kernel, 1)(rows, s_1, rest_s), SEQ, up)
    a_2 = lax.ppermute(advance("spread_a", spread_rest_kernel, MIRROR[1])(rows, a_1, rest_a), SEQ, down)
    middle = call(
        middle_kernel,
        shape(ROWS, 256),
        140_000_000,
        4 << 20,
        in_specs=[SMEM] + [VMEM] * 7,
        out_specs=VMEM,
        name="middle",
    )(turn, s_0, a_0, s_1, a_1, xw, gw, near)
    one = outer_part(1, s_1, a_1)
    s_2, a_2, middle, one, own = lax.optimization_barrier((s_2, a_2, middle, one, own))
    keep, send = call(
        far_kernel,
        (shape(16, 128, 256),) * 2,
        400_000_000,
        7 << 20,
        in_specs=[SMEM] * 2 + [VMEM] * 6,
        out_specs=(VMEM,) * 2,
        name="far",
    )(turn, core, s_2, a_2, xw, gw, middle, tok_t)
    got = lax.ppermute(send, "c", [(0, 1), (1, 0)])
    gx, step_grad, rates = call(
        finish_kernel,
        (shape(ROWS, width, dtype=BF), shape(HEADS, ROWS), shape(8, 256)),
        500_000_000,
        6 << 20,
        in_specs=[SMEM] + [VMEM] * 22,
        out_specs=(VMEM,) * 3,
        scratch_shapes=[pltpu.VMEM((PAIRS, 128), F32)],
        name="finish",
    )(turn, s_0, a_2, s_2, a_0, x, g, u, c, dt, bc, *one, *own, t_rows, s_cols, logit, rate)
    joined = call(
        join_kernel,
        shape(16, 136, 256),
        1_000_000,
        6 << 20,
        in_specs=[VMEM] * 3,
        out_specs=VMEM,
        name="join",
    )(keep, got, rates)
    folded = call(
        fold_kernel,
        shape(8, 24, 256),
        1_000_000,
        2 << 20,
        in_specs=[VMEM],
        out_specs=VMEM,
        name="fold",
    )(lax.all_to_all(joined, ("x", "y"), 0, 0))
    summed = call(
        last_kernel,
        shape(8, 24, 256),
        1_000_000,
        1 << 20,
        in_specs=[VMEM],
        out_specs=VMEM,
        name="last",
    )(lax.all_to_all(folded, ("quad", "turn"), 0, 0))
    last = lax.all_to_all(summed, ("y", "c"), 0, 0)
    rate_grad = last[0, 16, :HEADS] + last[1, 16, :HEADS]
    return gx[None], step_grad.T[None], rate_grad, last[:, :16].reshape(ROWS, 256)


def solution(mesh):
    devices = mesh.devices.reshape(4, 2, 4, 4, 2)
    parts = Mesh(devices, ("x", "quad", "turn", "y", "c"))
    rows = P(("y", "c"), SEQ, None)
    return jax.shard_map(
        shards,
        mesh=parts,
        in_specs=(rows, P(), rows, rows, P(), rows),
        out_specs=(rows, rows, P(), P(SEQ, None)),
        check_vma=False,
    )
```

```python
import functools

import jax
import jax.numpy as jnp
from jax import lax
from jax.experimental import pallas as pl
from jax.experimental.pallas import tpu as pltpu
from jax.sharding import Mesh
from jax.sharding import PartitionSpec as P

ROWS = 128
HEADS = 64
SLOTS = 4
PART = HEADS // SLOTS
PAIRS = PART // 2
ALL_PAIRS = HEADS // 2
TILE = PAIRS * 128
MIRROR = (2, 1, 0, 3)
GROUP = 8
GROUPS = HEADS // GROUP
BF = jnp.bfloat16
F32 = jnp.float32
NN = (((1,), (0,)), ((), ()))
NT = (((1,), (1,)), ((), ()))
TN = (((0,), (0,)), ((), ()))
HIGH = lax.Precision.HIGHEST
VMEM = pl.BlockSpec(memory_space=pltpu.VMEM)
SMEM = pl.BlockSpec(memory_space=pltpu.SMEM)
HBM = pl.BlockSpec(memory_space=pltpu.HBM)
SEQ = ("x", "quad", "turn")
BLOCK = ("x", "quad")
CHUNKS = 4
CHUNK = 1024


def iota(shape, dim):
    return lax.broadcasted_iota(jnp.int32, shape, dim)


def dot(a, b, dims=NN):
    return lax.dot_general(a, b, dims, preferred_element_type=F32)


def dot_exact(a, b):
    return lax.dot_general(a, b, NN, precision=HIGH, preferred_element_type=F32)


def dot_split(a, b):
    head = a.astype(BF)
    tail = (a - head.astype(F32)).astype(BF)
    return dot(head, b) + dot(tail, b)


def spread(cols, pair, left):
    one = cols[:, 2 * pair : 2 * pair + 1]
    two = cols[:, 2 * pair + 1 : 2 * pair + 2]
    return jnp.where(left, one, two)


def turned(values, turn):
    parts = [values[:, PART * k : PART * k + PART] for k in range(SLOTS)]
    out = values
    for t in range(SLOTS):
        order = jnp.concatenate([parts[(t + 3 - k) % SLOTS] for k in range(SLOTS)], axis=1)
        out = jnp.where(turn == t, order, out)
    return out


def lanes(pair, turn):
    slot, place = divmod(pair, PAIRS)
    start = lax.rem(turn + 3 - slot, SLOTS) * TILE + 128 * place
    return pl.ds(pl.multiple_of(start, 128), 128)


def tile(place):
    return slice(128 * place, 128 * place + 128)


def call(kernel, outs, flops, moved, room=8, **more):
    return pl.pallas_call(
        kernel,
        out_shape=outs,
        compiler_params=pltpu.CompilerParams(vmem_limit_bytes=room << 20),
        cost_estimate=pl.CostEstimate(flops=flops, bytes_accessed=moved, transcendentals=0),
        **more,
    )


def shape(*dims, dtype=F32):
    return jax.ShapeDtypeStruct(dims, dtype)


def advance(name, kernel, *fixed):
    return call(
        functools.partial(kernel, *fixed),
        shape(TILE + PAIRS if kernel is gather_step_kernel else TILE, 128),
        1_000_000,
        2 << 20,
        in_specs=[VMEM] * 3,
        out_specs=VMEM,
        name=name,
    )


def turn_kernel(core_ref, tok, mine, other):
    first = core_ref[0] == 0
    for i in range(32):
        part = tok[:, tile(i)].astype(F32).T
        x, z = divmod(i, 8)
        for y in range(4):
            one = part[32 * y : 32 * y + 16, :]
            two = part[32 * y + 16 : 32 * y + 32, :]
            rows = slice(512 * x + 128 * y + 16 * z, 512 * x + 128 * y + 16 * z + 16)
            mine[rows, :] = jnp.where(first, one, two).astype(BF)
            other[rows, :] = jnp.where(first, two, one)


def narrow_kernel(wide, out):
    out[...] = wide[...].astype(BF)


def project_kernel(
    turn_ref, logit, rate, tok_hbm, proj_hbm, x_hbm, bc_ref, c_ref, dt_ref, rows_ref, xw_ref, send, tok, proj, x, sems
):
    copies = []
    for k in range(CHUNKS):
        at = pl.ds(k * CHUNK, CHUNK)
        copies.append(
            (
                pltpu.make_async_copy(tok_hbm.at[:, at], tok.at[:, at], sems.at[0, k]),
                pltpu.make_async_copy(proj_hbm.at[at, :], proj.at[at, :], sems.at[1, k]),
            )
        )
        for copy in copies[-1]:
            copy.start()
    fetch_x = pltpu.make_async_copy(x_hbm, x, sems.at[2, 0])
    fetch_x.start()
    turn = turn_ref[0]
    z = turned(logit[...].T, turn)
    dt = jnp.maximum(z, 0.0) + jnp.log1p(jnp.exp(-jnp.abs(z)))
    a = -turned(rate[...], turn) * dt
    lower = (iota((ROWS, ROWS), 0) >= iota((ROWS, ROWS), 1)).astype(F32)
    c = dot_exact(lower, a)
    c_ref[...] = c
    dt_ref[...] = dt
    last = c[ROWS - 1 : ROWS, :]
    to_end = jnp.exp(last - c) * dt
    left = iota((ROWS, 128), 1) < 64
    left1 = iota((1, 128), 1) < 64
    for pair in range(ALL_PAIRS):
        rows_ref[pair : pair + 1, :] = spread(last, pair, left1)
    send[TILE : TILE + PAIRS, :] = rows_ref[0:PAIRS, :]
    total = jnp.zeros((ROWS, 256), F32)
    for k in range(CHUNKS):
        for copy in copies[k]:
            copy.wait()
        at = slice(k * CHUNK, k * CHUNK + CHUNK)
        total = total + dot(tok[:, at], proj[at, :])
    bc = total.astype(BF)
    bc_ref[...] = bc
    b_t = bc[:, :128].astype(F32).T.astype(BF)
    fetch_x.wait()
    for pair in range(ALL_PAIRS):
        at = lanes(pair, turn)
        xw = (x[:, at].astype(F32) * spread(to_end, pair, left)).astype(BF)
        xw_ref[:, at] = xw
        if pair < PAIRS:
            send[tile(pair), :] = dot(b_t, xw)


def adjoint_kernel(turn_ref, bc, c_ref, rows, g, gw_ref, send):
    turn = turn_ref[0]
    ec = jnp.exp(c_ref[...])
    c_t = bc[:, 128:].astype(F32).T.astype(BF)
    left = iota((ROWS, 128), 1) < 64
    first = MIRROR[0] * PAIRS
    for pair in range(ALL_PAIRS):
        at = lanes(pair, turn)
        gw = (g[:, at].astype(F32) * spread(ec, pair, left)).astype(BF)
        gw_ref[:, at] = gw
        if first <= pair < first + PAIRS:
            send[tile(pair - first), :] = dot(c_t, gw)
    send[TILE : TILE + PAIRS, :] = rows[first : first + PAIRS, :]


def rest_kernel(turn_ref, bc, c_ref, dt_ref, xw, gw, rest_s, rest_a, cg_ref, dtg_ref, ct_ref):
    turn = turn_ref[0]
    both = bc[...].astype(F32)
    b_t = both[:, :128].T.astype(BF)
    c_t = both[:, 128:].T.astype(BF)
    for k in range(1, SLOTS):
        for place in range(PAIRS):
            rest_s[k - 1, tile(place), :] = dot(b_t, xw[:, lanes(k * PAIRS + place, turn)])
            rest_a[k - 1, tile(place), :] = dot(c_t, gw[:, lanes(MIRROR[k] * PAIRS + place, turn)])
    c = c_ref[...]
    ct_ref[...] = c.T
    for group in range(GROUPS):
        cg_ref[group] = c[:, GROUP * group : GROUP * group + GROUP]
        dtg_ref[group] = dt_ref[:, GROUP * group : GROUP * group + GROUP]


def gather_step_kernel(slot, k, rows, got, rest, out):
    for place in range(PAIRS):
        own = rows[slot * PAIRS + place : slot * PAIRS + place + 1, :]
        out[tile(place), :] = jnp.exp(own) * got[tile(place), :] + rest[k - 1, tile(place), :]
    out[TILE : TILE + PAIRS, :] = got[TILE : TILE + PAIRS, :] + rows[slot * PAIRS : slot * PAIRS + PAIRS, :]


def spread_step_kernel(slot, rows, state, local, out):
    for place in range(PAIRS):
        own = rows[slot * PAIRS + place : slot * PAIRS + place + 1, :]
        out[tile(place), :] = jnp.exp(own) * state[tile(place), :] + local[tile(place), :]


def spread_rest_kernel(slot, rows, state, rest, out):
    spread_step_kernel(slot, rows, state, rest.at[0], out)


def intra_kernel(turn_ref, bc, cg, dtg, ct, x, g, u_ref, t_ref, s_ref, ds_ref):
    @pl.when(pl.program_id(0) == 0)
    def _():
        ds_ref[...] = jnp.zeros_like(ds_ref)

    sc_t = dot(bc[:, :128], bc[:, 128:], NT)
    causal = iota((ROWS, ROWS), 0) <= iota((ROWS, ROWS), 1)
    left = iota((ROWS, 128), 1) < 64
    ones = (left.astype(F32).astype(BF), (1.0 - left.astype(F32)).astype(BF))
    lane8 = iota((ROWS, GROUP), 1)
    s_all = jnp.zeros((ROWS, GROUP), F32)
    total = ds_ref[...]
    for pair in range(GROUP // 2):
        xs = x[:, 128 * pair : 128 * pair + 128]
        gs = g[:, 128 * pair : 128 * pair + 128]
        parts = []
        for side in range(2):
            h = 2 * pair + side
            gx = dot(xs * ones[side], gs, NT)
            gap = ct[h : h + 1, :] - cg[0, :, h : h + 1]
            decay = jnp.exp(jnp.where(causal, gap, -jnp.inf))
            parts.append(dot((decay * sc_t).astype(BF), gs))
            p = decay * gx * dtg[0, :, h : h + 1]
            total = total + p
            m = p * sc_t
            t_ref[h : h + 1, :] = jnp.sum(m, axis=0, keepdims=True)
            s_all = jnp.where(lane8 == h, jnp.sum(m, axis=1, keepdims=True), s_all)
        u_ref[:, 128 * pair : 128 * pair + 128] = jnp.where(left, parts[0], parts[1])
    s_ref[0] = s_all
    ds_ref[...] = total


def combine_kernel(rows, rest_s, rest_a, got_s, got_a, msg):
    for place in range(PAIRS):
        own = rows[3 * PAIRS + place : 3 * PAIRS + place + 1, :]
        decay = jnp.exp(own)
        msg[place, 0:128, :] = decay * got_s[tile(place), :] + rest_s[2, tile(place), :]
        msg[place, 128:256, :] = decay * got_a[tile(place), :] + rest_a[2, tile(place), :]
        msg[place, 256:257, :] = own + got_s[TILE + place : TILE + place + 1, :]
        msg[place, 257:258, :] = own + got_a[TILE + place : TILE + place + 1, :]
        msg[place, 258:264, :] = jnp.zeros((6, 128), F32)


def scan_kernel(msg, out):
    state = jnp.zeros((128, 128), F32)
    for i in range(PAIRS):
        out[i, 0:128, :] = state
        state = jnp.exp(msg[i, 256:257, :]) * state + msg[i, 0:128, :]
    state = jnp.zeros((128, 128), F32)
    for i in range(PAIRS - 1, -1, -1):
        out[i, 128:256, :] = state
        state = jnp.exp(msg[i, 257:258, :]) * state + msg[i, 128:256, :]


def near_states(got_s, got_a, back, place):
    mark = TILE + place
    state = jnp.exp(got_s[mark : mark + 1, :]) * back[place, 0:128, :] + got_s[tile(place), :]
    adj = jnp.exp(got_a[mark : mark + 1, :]) * back[place, 128:256, :] + got_a[tile(place), :]
    return state, adj


def unfold_kernel(rows, rest_s, rest_a, got_s, got_a, back, s_next, a_next):
    for place in range(PAIRS):
        state, adj = near_states(got_s, got_a, back, place)
        decay = jnp.exp(rows[3 * PAIRS + place : 3 * PAIRS + place + 1, :])
        s_next[tile(place), :] = decay * state + rest_s[2, tile(place), :]
        a_next[tile(place), :] = decay * adj + rest_a[2, tile(place), :]


def outer_terms(slot, turn, s_in, a_in, x, g, u, c_ref, dt_ref, bc, dots, store):
    cols = slice(PART * slot, PART * slot + PART)
    c = c_ref[:, cols]
    dt = dt_ref[:, cols]
    last = c[ROWS - 1 : ROWS, :]
    end = jnp.exp(last - c)
    ec = jnp.exp(c)
    b_bf, c_bf = bc[:, :128], bc[:, 128:]
    left = iota((ROWS, 128), 1) < 64
    choice = iota((ROWS, PART), 1) - (iota((ROWS, PART), 0) >= 64).astype(jnp.int32)
    role = jnp.zeros((ROWS, PART), F32)
    outer = jnp.zeros((ROWS, PART), F32)
    for place in range(PAIRS):
        at = lanes(slot * PAIRS + place, turn)
        picked = (choice == 2 * place).astype(F32).astype(BF)
        state = s_in[tile(place), :]
        adj = a_in[tile(place), :]
        dots[place : place + 1, :] = jnp.sum(adj * state, axis=0, keepdims=True)
        gw = g[:, at].astype(F32) * spread(ec, place, left)
        role = role + dot_split(gw * dot(c_bf, state.astype(BF)), picked)
        add = dot(b_bf, adj.astype(BF)) * spread(end, place, left)
        store(place, ((u[:, at] + add) * spread(dt, place, left)).astype(BF))
        outer = outer + dot_split(x[:, at].astype(F32) * add, picked)
    row, col = iota((128, PART), 0), iota((128, PART), 1)
    side = ((row >= 64).astype(jnp.int32) == col % 2).astype(F32)
    both = dot_exact(dots[...], side)
    mine = iota((PAIRS, PART), 0) == iota((PAIRS, PART), 1) // 2
    meet = jnp.exp(last) * jnp.sum(jnp.where(mine, both, 0.0), axis=0, keepdims=True)
    return role, outer, meet


def outer_kernel(
    slot, turn_ref, s_in, a_in, x, g, u, c_ref, dt_ref, bc, gx_ref, role_ref, outer_ref, meet_ref, dots
):
    def store(place, value):
        gx_ref[:, tile(place)] = value

    role, outer, meet = outer_terms(slot, turn_ref[0], s_in, a_in, x, g, u, c_ref, dt_ref, bc, dots, store)
    role_ref[...] = role
    outer_ref[...] = outer
    meet_ref[...] = jnp.broadcast_to(meet, (8, PART))


def near_kernel(turn_ref, got_s, got_a, back, xw, gw, bc, ds, out, s_own, a_own):
    turn = turn_ref[0]
    inner = ds[...].astype(BF)
    grad_b = dot(inner, bc[:, 128:])
    grad_c = dot(inner, bc[:, :128], TN)
    for place in range(PAIRS):
        at = lanes(3 * PAIRS + place, turn)
        state, adj = near_states(got_s, got_a, back, place)
        s_own[tile(place), :] = state
        a_own[tile(place), :] = adj
        grad_b = grad_b + dot(xw[:, at], adj.astype(BF), NT)
        grad_c = grad_c + dot(gw[:, at], state.astype(BF), NT)
    out[:, :128] = grad_b
    out[:, 128:] = grad_c


def more_terms(turn, k, s_in, a_in, xw, gw, grad_b, grad_c):
    for place in range(PAIRS):
        grad_b = grad_b + dot(xw[:, lanes(MIRROR[k] * PAIRS + place, turn)], a_in[tile(place), :].astype(BF), NT)
        grad_c = grad_c + dot(gw[:, lanes(k * PAIRS + place, turn)], s_in[tile(place), :].astype(BF), NT)
    return grad_b, grad_c


def middle_kernel(turn_ref, s_0, a_0, s_1, a_1, xw, gw, near, out):
    turn = turn_ref[0]
    grads = near[:, :128], near[:, 128:]
    grads = more_terms(turn, 0, s_0, a_0, xw, gw, *grads)
    grads = more_terms(turn, 1, s_1, a_1, xw, gw, *grads)
    out[:, :128] = grads[0]
    out[:, 128:] = grads[1]


def far_kernel(turn_ref, s_in, a_in, xw, gw, near, out):
    grad_b, grad_c = more_terms(turn_ref[0], 2, s_in, a_in, xw, gw, near[:, :128], near[:, 128:])
    out[:, :128] = grad_b.astype(BF).astype(F32)
    out[:, 128:] = grad_c.astype(BF).astype(F32)


def weight_kernel(tok_mine, tok_got, mine, got, msg):
    here, there = mine[...].astype(BF), got[...].astype(BF)
    for k in range(16):
        msg[k] = dot(tok_mine[tile(k), :], here) + dot(tok_got[tile(k), :], there)


def fold_kernel(msg, rates, one, two, three, out):
    total = msg[0]
    for k in range(1, 16):
        total = total + msg[k]
    for z in range(8):
        out[z, 0:16, :] = total[16 * z : 16 * z + 16, :]
        out[z, 16:24, :] = rates[...] + one[...] + two[...] + three[...]


def last_kernel(msg, out):
    total = msg[0]
    for k in range(1, 8):
        total = total + msg[k]
    for k in range(8):
        out[k] = total


def finish_kernel(
    turn_ref, s_0, a_0, s_2, a_2, x, g, u, c_ref, dt_ref, bc, gx_1, role_1, outer_1, meet_1, gx_3, role_3, outer_3,
    meet_3, t_rows, s_cols, logit, rate, gx_ref, step_ref, rate_ref, dots,
):
    turn = turn_ref[0]

    def terms(slot, state, adj):
        def store(place, value):
            gx_ref[:, lanes(slot * PAIRS + place, turn)] = value

        return outer_terms(slot, turn, state, adj, x, g, u, c_ref, dt_ref, bc, dots, store)

    zero, two = terms(0, s_0, a_0), terms(2, s_2, a_2)
    for place in range(PAIRS):
        gx_ref[:, lanes(PAIRS + place, turn)] = gx_1[:, tile(place)]
        gx_ref[:, lanes(3 * PAIRS + place, turn)] = gx_3[:, tile(place)]
    dt = dt_ref[...]
    role_t = jnp.concatenate([zero[0], role_1[...], two[0], role_3[...]], axis=1) + t_rows[...].T
    outer = jnp.concatenate([zero[1], outer_1[...], two[1], outer_3[...]], axis=1)
    meet = jnp.concatenate([zero[2], meet_1[0:1, :], two[2], meet_3[0:1, :]], axis=1)
    role_s = jnp.concatenate([s_cols[k] for k in range(GROUPS)], axis=1)
    row, col = iota((ROWS, ROWS), 0), iota((ROWS, ROWS), 1)
    later = (col >= row).astype(F32)
    before = (col < row).astype(F32)
    da = dot_exact(later, role_t - role_s) + dot_exact(before, outer * dt) + meet
    ddt = turned(role_s / dt + outer, turn) - rate[...] * turned(da, turn)
    step_ref[...] = ddt.T / (1.0 + jnp.exp(-logit[...]))
    rate_row = turned(-jnp.sum(dt * da, axis=0, keepdims=True), turn)
    wide = jnp.concatenate([rate_row, jnp.zeros((1, 256 - HEADS), F32)], axis=1)
    rate_ref[...] = jnp.broadcast_to(wide, (8, 256))


def shards(layer_input, projection, ssm_input, step_logit, decay_rate, output_grad):
    tok, x, g, logit = layer_input[0], ssm_input[0], output_grad[0], step_logit[0].T
    rate = decay_rate[None, :]
    width = x.shape[1]
    turn = lax.axis_index("turn").astype(jnp.int32)[None]
    core = lax.axis_index("c").astype(jnp.int32)[None]
    up = [(i, i + 1) for i in range(31)]
    down = [(i + 1, i) for i in range(31)]

    bc, c, dt, rows, xw, send_s = call(
        project_kernel,
        (
            shape(ROWS, 256, dtype=BF),
            shape(ROWS, HEADS),
            shape(ROWS, HEADS),
            shape(ALL_PAIRS, 128),
            shape(ROWS, width, dtype=BF),
            shape(TILE + PAIRS, 128),
        ),
        400_000_000,
        6 << 20,
        room=52,
        in_specs=[SMEM, VMEM, VMEM, HBM, HBM, HBM],
        out_specs=(VMEM,) * 6,
        scratch_shapes=[
            pltpu.VMEM((ROWS, width), BF),
            pltpu.VMEM((width, 256), BF),
            pltpu.VMEM((ROWS, width), BF),
            pltpu.SemaphoreType.DMA((3, CHUNKS)),
        ],
        name="project",
    )(turn, logit, rate, tok, projection, x)
    got_s = lax.ppermute(send_s, SEQ, up)
    gw, send_a = call(
        adjoint_kernel,
        (shape(ROWS, width, dtype=BF), shape(TILE + PAIRS, 128)),
        140_000_000,
        3 << 20,
        in_specs=[SMEM] + [VMEM] * 4,
        out_specs=(VMEM,) * 2,
        name="adjoint",
    )(turn, bc, c, rows, g)
    got_a = lax.ppermute(send_a, SEQ, down)

    rest_s, rest_a, cg, dtg, ct = call(
        rest_kernel,
        (
            shape(3, TILE, 128),
            shape(3, TILE, 128),
            shape(GROUPS, ROWS, GROUP),
            shape(GROUPS, ROWS, GROUP),
            shape(HEADS, ROWS),
        ),
        200_000_000,
        6 << 20,
        in_specs=[SMEM] + [VMEM] * 5,
        out_specs=(VMEM,) * 5,
        name="rest",
    )(turn, bc, c, dt, xw, gw)
    tok_mine, tok_other = call(
        turn_kernel,
        (shape(width // 2, ROWS, dtype=BF), shape(width // 2, ROWS)),
        1_000_000,
        3 << 20,
        in_specs=[SMEM, VMEM],
        out_specs=(VMEM,) * 2,
        name="turn",
    )(core, tok)
    swap = [(0, 1), (1, 0)]
    tok_got = call(
        narrow_kernel,
        shape(width // 2, ROWS, dtype=BF),
        1_000_000,
        2 << 20,
        in_specs=[VMEM],
        out_specs=VMEM,
        name="narrow",
    )(lax.ppermute(tok_other, "c", swap))

    wide = GROUP * 64

    def place(i, turn):
        return lax.rem(turn[0] + 3 - i // 2, SLOTS) * 2 + i % 2

    u, t_rows, s_cols, ds = call(
        intra_kernel,
        (
            shape(ROWS, width),
            shape(HEADS, ROWS),
            shape(GROUPS, ROWS, GROUP),
            shape(ROWS, ROWS),
        ),
        800_000_000,
        20 << 20,
        grid_spec=pltpu.PrefetchScalarGridSpec(
            num_scalar_prefetch=1,
            grid=(GROUPS,),
            in_specs=[
                pl.BlockSpec((ROWS, 256), lambda i, turn: (0, 0)),
                pl.BlockSpec((1, ROWS, GROUP), lambda i, turn: (i, 0, 0)),
                pl.BlockSpec((1, ROWS, GROUP), lambda i, turn: (i, 0, 0)),
                pl.BlockSpec((GROUP, ROWS), lambda i, turn: (i, 0)),
                pl.BlockSpec((ROWS, wide), lambda i, turn: (0, place(i, turn))),
                pl.BlockSpec((ROWS, wide), lambda i, turn: (0, place(i, turn))),
            ],
            out_specs=(
                pl.BlockSpec((ROWS, wide), lambda i, turn: (0, place(i, turn))),
                pl.BlockSpec((GROUP, ROWS), lambda i, turn: (i, 0)),
                pl.BlockSpec((1, ROWS, GROUP), lambda i, turn: (i, 0, 0)),
                pl.BlockSpec((ROWS, ROWS), lambda i, turn: (0, 0)),
            ),
        ),
        name="intra",
    )(turn, bc, cg, dtg, ct, x, g)
    for k in (1, 2):
        got_s = lax.ppermute(advance("gather_s", gather_step_kernel, k, k)(rows, got_s, rest_s), SEQ, up)
        got_a = lax.ppermute(advance("gather_a", gather_step_kernel, MIRROR[k], k)(rows, got_a, rest_a), SEQ, down)
    got_s, got_a, u, tok_mine, tok_got = lax.optimization_barrier((got_s, got_a, u, tok_mine, tok_got))

    sent = call(
        combine_kernel,
        shape(PAIRS, 264, 128),
        4_000_000,
        4 << 20,
        in_specs=[VMEM] * 5,
        out_specs=VMEM,
        name="combine",
    )(rows, rest_s, rest_a, got_s, got_a)
    held = lax.all_to_all(sent, BLOCK, 0, 0)
    scanned = call(
        scan_kernel,
        shape(PAIRS, 256, 128),
        4_000_000,
        4 << 20,
        in_specs=[VMEM],
        out_specs=VMEM,
        name="scan",
    )(held)
    back = lax.all_to_all(scanned, BLOCK, 0, 0)
    s_next, a_next = call(
        unfold_kernel,
        (shape(TILE, 128),) * 2,
        8_000_000,
        4 << 20,
        in_specs=[VMEM] * 6,
        out_specs=(VMEM,) * 2,
        name="unfold",
    )(rows, rest_s, rest_a, got_s, got_a, back)
    s_0 = lax.ppermute(s_next, SEQ, up)
    a_0 = lax.ppermute(a_next, SEQ, down)
    near, s_own, a_own = call(
        near_kernel,
        (shape(ROWS, 256), shape(TILE, 128), shape(TILE, 128)),
        140_000_000,
        4 << 20,
        in_specs=[SMEM] + [VMEM] * 7,
        out_specs=(VMEM,) * 3,
        name="near",
    )(turn, got_s, got_a, back, xw, gw, bc, ds)

    def outer_part(slot, state, adj):
        return call(
            functools.partial(outer_kernel, slot),
            (
                shape(ROWS, TILE, dtype=BF),
                shape(ROWS, PART),
                shape(ROWS, PART),
                shape(8, PART),
            ),
            250_000_000,
            6 << 20,
            in_specs=[SMEM] + [VMEM] * 8,
            out_specs=(VMEM,) * 4,
            scratch_shapes=[pltpu.VMEM((PAIRS, 128), F32)],
            name="outer",
        )(turn, state, adj, x, g, u, c, dt, bc)

    own = outer_part(3, s_own, a_own)
    s_1 = lax.ppermute(advance("spread_s", spread_step_kernel, 0)(rows, s_0, send_s), SEQ, up)
    a_1 = lax.ppermute(advance("spread_a", spread_step_kernel, MIRROR[0])(rows, a_0, send_a), SEQ, down)
    s_2 = lax.ppermute(advance("spread_s", spread_rest_kernel, 1)(rows, s_1, rest_s), SEQ, up)
    a_2 = lax.ppermute(advance("spread_a", spread_rest_kernel, MIRROR[1])(rows, a_1, rest_a), SEQ, down)
    middle = call(
        middle_kernel,
        shape(ROWS, 256),
        140_000_000,
        4 << 20,
        in_specs=[SMEM] + [VMEM] * 7,
        out_specs=VMEM,
        name="middle",
    )(turn, s_0, a_0, s_1, a_1, xw, gw, near)
    one = outer_part(1, s_1, a_1)
    s_2, a_2, middle, one, own = lax.optimization_barrier((s_2, a_2, middle, one, own))
    part = call(
        far_kernel,
        shape(ROWS, 256),
        70_000_000,
        3 << 20,
        in_specs=[SMEM] + [VMEM] * 5,
        out_specs=VMEM,
        name="far",
    )(turn, s_2, a_2, xw, gw, middle)
    weight = call(
        weight_kernel,
        shape(16, 128, 256),
        300_000_000,
        4 << 20,
        in_specs=[VMEM] * 4,
        out_specs=VMEM,
        name="weight",
    )(tok_mine, tok_got, part, lax.ppermute(part, "c", swap))
    weight, s_2, a_2 = lax.optimization_barrier((weight, s_2, a_2))
    over_xy = lax.all_to_all(weight, ("x", "y"), 0, 0)
    gx, step_grad, rates = call(
        finish_kernel,
        (shape(ROWS, width, dtype=BF), shape(HEADS, ROWS), shape(8, 256)),
        500_000_000,
        6 << 20,
        in_specs=[SMEM] + [VMEM] * 22,
        out_specs=(VMEM,) * 3,
        scratch_shapes=[pltpu.VMEM((PAIRS, 128), F32)],
        name="finish",
    )(turn, s_0, a_2, s_2, a_0, x, g, u, c, dt, bc, *one, *own, t_rows, s_cols, logit, rate)
    far_rates = [lax.ppermute(rates, "x", [(i, (i + hop) % 4) for i in range(4)]) for hop in (1, 2, 3)]
    folded = call(
        fold_kernel,
        shape(8, 24, 256),
        1_000_000,
        2 << 20,
        in_specs=[VMEM] * 5,
        out_specs=VMEM,
        name="fold",
    )(over_xy, rates, *far_rates)
    summed = call(
        last_kernel,
        shape(8, 24, 256),
        1_000_000,
        1 << 20,
        in_specs=[VMEM],
        out_specs=VMEM,
        name="last",
    )(lax.all_to_all(folded, ("quad", "turn"), 0, 0))
    last = lax.all_to_all(summed, ("y", "c"), 0, 0)
    rate_grad = jnp.sum(last[:, 16, :HEADS], axis=0)
    return gx[None], step_grad.T[None], rate_grad, last[:, :16].reshape(ROWS, 256)


def solution(mesh):
    devices = mesh.devices.reshape(4, 2, 4, 4, 2)
    parts = Mesh(devices, ("x", "quad", "turn", "y", "c"))
    rows = P(("y", "c"), SEQ, None)
    return jax.shard_map(
        shards,
        mesh=parts,
        in_specs=(rows, P(), rows, rows, P(), rows),
        out_specs=(rows, rows, P(), P(SEQ, None)),
        check_vma=False,
    )
```

```python
import functools

import jax
import jax.numpy as jnp
from jax import lax
from jax.experimental import pallas as pl
from jax.experimental.pallas import tpu as pltpu
from jax.sharding import Mesh
from jax.sharding import PartitionSpec as P

ROWS = 128
HEADS = 64
SLOTS = 4
PART = HEADS // SLOTS
PAIRS = PART // 2
ALL_PAIRS = HEADS // 2
TILE = PAIRS * 128
MIRROR = (2, 1, 0, 3)
GROUP = 8
GROUPS = HEADS // GROUP
BF = jnp.bfloat16
F32 = jnp.float32
NN = (((1,), (0,)), ((), ()))
NT = (((1,), (1,)), ((), ()))
TN = (((0,), (0,)), ((), ()))
HIGH = lax.Precision.HIGHEST
VMEM = pl.BlockSpec(memory_space=pltpu.VMEM)
SMEM = pl.BlockSpec(memory_space=pltpu.SMEM)
HBM = pl.BlockSpec(memory_space=pltpu.HBM)
SEQ = ("x", "quad", "turn")
BLOCK = ("x", "quad")
CHUNKS = 4
CHUNK = 1024


def iota(shape, dim):
    return lax.broadcasted_iota(jnp.int32, shape, dim)


def dot(a, b, dims=NN):
    return lax.dot_general(a, b, dims, preferred_element_type=F32)


def dot_exact(a, b):
    return lax.dot_general(a, b, NN, precision=HIGH, preferred_element_type=F32)


def dot_split(a, b):
    head = a.astype(BF)
    tail = (a - head.astype(F32)).astype(BF)
    return dot(head, b) + dot(tail, b)


def spread(cols, pair, left):
    one = cols[:, 2 * pair : 2 * pair + 1]
    two = cols[:, 2 * pair + 1 : 2 * pair + 2]
    return jnp.where(left, one, two)


def turned(values, turn):
    parts = [values[:, PART * k : PART * k + PART] for k in range(SLOTS)]
    out = values
    for t in range(SLOTS):
        order = jnp.concatenate([parts[(t + 3 - k) % SLOTS] for k in range(SLOTS)], axis=1)
        out = jnp.where(turn == t, order, out)
    return out


def lanes(pair, turn):
    slot, place = divmod(pair, PAIRS)
    start = lax.rem(turn + 3 - slot, SLOTS) * TILE + 128 * place
    return pl.ds(pl.multiple_of(start, 128), 128)


def tile(place):
    return slice(128 * place, 128 * place + 128)


def call(kernel, outs, flops, moved, room=8, **more):
    return pl.pallas_call(
        kernel,
        out_shape=outs,
        compiler_params=pltpu.CompilerParams(vmem_limit_bytes=room << 20),
        cost_estimate=pl.CostEstimate(flops=flops, bytes_accessed=moved, transcendentals=0),
        **more,
    )


def shape(*dims, dtype=F32):
    return jax.ShapeDtypeStruct(dims, dtype)


def advance(name, kernel, *fixed):
    return call(
        functools.partial(kernel, *fixed),
        shape(TILE + PAIRS if kernel is gather_step_kernel else TILE, 128),
        1_000_000,
        2 << 20,
        in_specs=[VMEM] * 3,
        out_specs=VMEM,
        name=name,
    )


def turn_kernel(place_ref, tok, *refs):
    y, core = place_ref[1], place_ref[2]
    outs, held = refs[:8], refs[8]
    for i in range(32):
        held[...] = tok[:, tile(i)].astype(F32).T
        for hop in range(4):
            for side in range(2):
                start = lax.rem(y + hop, 4) * 32 + lax.rem(core + side, 2) * 16
                outs[4 * side + hop][16 * i : 16 * i + 16, :] = held[pl.ds(pl.multiple_of(start, 16), 16), :]


def narrow_kernel(*refs):
    for k in range(8):
        refs[8][k] = refs[k][...].astype(BF)


def project_kernel(
    turn_ref, logit, rate, tok_hbm, proj_hbm, x_hbm, bc_ref, c_ref, dt_ref, rows_ref, xw_ref, send, tok, proj, x, sems
):
    copies = []
    for k in range(CHUNKS):
        at = pl.ds(k * CHUNK, CHUNK)
        copies.append(
            (
                pltpu.make_async_copy(tok_hbm.at[:, at], tok.at[:, at], sems.at[0, k]),
                pltpu.make_async_copy(proj_hbm.at[at, :], proj.at[at, :], sems.at[1, k]),
            )
        )
        for copy in copies[-1]:
            copy.start()
    fetch_x = pltpu.make_async_copy(x_hbm, x, sems.at[2, 0])
    fetch_x.start()
    turn = turn_ref[0]
    z = turned(logit[...].T, turn)
    dt = jnp.maximum(z, 0.0) + jnp.log1p(jnp.exp(-jnp.abs(z)))
    a = -turned(rate[...], turn) * dt
    lower = (iota((ROWS, ROWS), 0) >= iota((ROWS, ROWS), 1)).astype(F32)
    c = dot_exact(lower, a)
    c_ref[...] = c
    dt_ref[...] = dt
    last = c[ROWS - 1 : ROWS, :]
    to_end = jnp.exp(last - c) * dt
    left = iota((ROWS, 128), 1) < 64
    left1 = iota((1, 128), 1) < 64
    for pair in range(ALL_PAIRS):
        rows_ref[pair : pair + 1, :] = spread(last, pair, left1)
    send[TILE : TILE + PAIRS, :] = rows_ref[0:PAIRS, :]
    total = jnp.zeros((ROWS, 256), F32)
    for k in range(CHUNKS):
        for copy in copies[k]:
            copy.wait()
        at = slice(k * CHUNK, k * CHUNK + CHUNK)
        total = total + dot(tok[:, at], proj[at, :])
    bc = total.astype(BF)
    bc_ref[...] = bc
    b_t = bc[:, :128].astype(F32).T.astype(BF)
    fetch_x.wait()
    for pair in range(ALL_PAIRS):
        at = lanes(pair, turn)
        xw = (x[:, at].astype(F32) * spread(to_end, pair, left)).astype(BF)
        xw_ref[:, at] = xw
        if pair < PAIRS:
            send[tile(pair), :] = dot(b_t, xw)


def adjoint_kernel(turn_ref, bc, c_ref, rows, g, gw_ref, send):
    turn = turn_ref[0]
    ec = jnp.exp(c_ref[...])
    c_t = bc[:, 128:].astype(F32).T.astype(BF)
    left = iota((ROWS, 128), 1) < 64
    first = MIRROR[0] * PAIRS
    for pair in range(ALL_PAIRS):
        at = lanes(pair, turn)
        gw = (g[:, at].astype(F32) * spread(ec, pair, left)).astype(BF)
        gw_ref[:, at] = gw
        if first <= pair < first + PAIRS:
            send[tile(pair - first), :] = dot(c_t, gw)
    send[TILE : TILE + PAIRS, :] = rows[first : first + PAIRS, :]


def rest_kernel(turn_ref, bc, c_ref, dt_ref, xw, gw, rest_s, rest_a, cg_ref, dtg_ref, ct_ref):
    turn = turn_ref[0]
    both = bc[...].astype(F32)
    b_t = both[:, :128].T.astype(BF)
    c_t = both[:, 128:].T.astype(BF)
    for k in range(1, SLOTS):
        for place in range(PAIRS):
            rest_s[k - 1, tile(place), :] = dot(b_t, xw[:, lanes(k * PAIRS + place, turn)])
            rest_a[k - 1, tile(place), :] = dot(c_t, gw[:, lanes(MIRROR[k] * PAIRS + place, turn)])
    c = c_ref[...]
    ct_ref[...] = c.T
    for group in range(GROUPS):
        cg_ref[group] = c[:, GROUP * group : GROUP * group + GROUP]
        dtg_ref[group] = dt_ref[:, GROUP * group : GROUP * group + GROUP]


def gather_step_kernel(slot, k, rows, got, rest, out):
    for place in range(PAIRS):
        own = rows[slot * PAIRS + place : slot * PAIRS + place + 1, :]
        out[tile(place), :] = jnp.exp(own) * got[tile(place), :] + rest[k - 1, tile(place), :]
    out[TILE : TILE + PAIRS, :] = got[TILE : TILE + PAIRS, :] + rows[slot * PAIRS : slot * PAIRS + PAIRS, :]


def spread_step_kernel(slot, rows, state, local, out):
    for place in range(PAIRS):
        own = rows[slot * PAIRS + place : slot * PAIRS + place + 1, :]
        out[tile(place), :] = jnp.exp(own) * state[tile(place), :] + local[tile(place), :]


def spread_rest_kernel(slot, rows, state, rest, out):
    spread_step_kernel(slot, rows, state, rest.at[0], out)


def intra_kernel(turn_ref, bc, cg, dtg, ct, x, g, u_ref, t_ref, s_ref, ds_ref):
    @pl.when(pl.program_id(0) == 0)
    def _():
        ds_ref[...] = jnp.zeros_like(ds_ref)

    sc_t = dot(bc[:, :128], bc[:, 128:], NT)
    causal = iota((ROWS, ROWS), 0) <= iota((ROWS, ROWS), 1)
    left = iota((ROWS, 128), 1) < 64
    ones = (left.astype(F32).astype(BF), (1.0 - left.astype(F32)).astype(BF))
    lane8 = iota((ROWS, GROUP), 1)
    s_all = jnp.zeros((ROWS, GROUP), F32)
    total = ds_ref[...]
    for pair in range(GROUP // 2):
        xs = x[:, 128 * pair : 128 * pair + 128]
        gs = g[:, 128 * pair : 128 * pair + 128]
        parts = []
        for side in range(2):
            h = 2 * pair + side
            gx = dot(xs * ones[side], gs, NT)
            gap = ct[h : h + 1, :] - cg[0, :, h : h + 1]
            decay = jnp.exp(jnp.where(causal, gap, -jnp.inf))
            parts.append(dot((decay * sc_t).astype(BF), gs))
            p = decay * gx * dtg[0, :, h : h + 1]
            total = total + p
            m = p * sc_t
            t_ref[h : h + 1, :] = jnp.sum(m, axis=0, keepdims=True)
            s_all = jnp.where(lane8 == h, jnp.sum(m, axis=1, keepdims=True), s_all)
        u_ref[:, 128 * pair : 128 * pair + 128] = jnp.where(left, parts[0], parts[1])
    s_ref[0] = s_all
    ds_ref[...] = total


def combine_kernel(rows, rest_s, rest_a, got_s, got_a, msg):
    for place in range(PAIRS):
        own = rows[3 * PAIRS + place : 3 * PAIRS + place + 1, :]
        decay = jnp.exp(own)
        msg[place, 0:128, :] = decay * got_s[tile(place), :] + rest_s[2, tile(place), :]
        msg[place, 128:256, :] = decay * got_a[tile(place), :] + rest_a[2, tile(place), :]
        msg[place, 256:257, :] = own + got_s[TILE + place : TILE + place + 1, :]
        msg[place, 257:258, :] = own + got_a[TILE + place : TILE + place + 1, :]
        msg[place, 258:264, :] = jnp.zeros((6, 128), F32)


def scan_kernel(msg, out):
    state = jnp.zeros((128, 128), F32)
    for i in range(PAIRS):
        out[i, 0:128, :] = state
        state = jnp.exp(msg[i, 256:257, :]) * state + msg[i, 0:128, :]
    state = jnp.zeros((128, 128), F32)
    for i in range(PAIRS - 1, -1, -1):
        out[i, 128:256, :] = state
        state = jnp.exp(msg[i, 257:258, :]) * state + msg[i, 128:256, :]


def near_states(got_s, got_a, back, place):
    mark = TILE + place
    state = jnp.exp(got_s[mark : mark + 1, :]) * back[place, 0:128, :] + got_s[tile(place), :]
    adj = jnp.exp(got_a[mark : mark + 1, :]) * back[place, 128:256, :] + got_a[tile(place), :]
    return state, adj


def unfold_kernel(rows, rest_s, rest_a, got_s, got_a, back, s_next, a_next):
    for place in range(PAIRS):
        state, adj = near_states(got_s, got_a, back, place)
        decay = jnp.exp(rows[3 * PAIRS + place : 3 * PAIRS + place + 1, :])
        s_next[tile(place), :] = decay * state + rest_s[2, tile(place), :]
        a_next[tile(place), :] = decay * adj + rest_a[2, tile(place), :]


def outer_terms(slot, turn, s_in, a_in, x, g, u, c_ref, dt_ref, bc, dots, store):
    cols = slice(PART * slot, PART * slot + PART)
    c = c_ref[:, cols]
    dt = dt_ref[:, cols]
    last = c[ROWS - 1 : ROWS, :]
    end = jnp.exp(last - c)
    ec = jnp.exp(c)
    b_bf, c_bf = bc[:, :128], bc[:, 128:]
    left = iota((ROWS, 128), 1) < 64
    choice = iota((ROWS, PART), 1) - (iota((ROWS, PART), 0) >= 64).astype(jnp.int32)
    role = jnp.zeros((ROWS, PART), F32)
    outer = jnp.zeros((ROWS, PART), F32)
    for place in range(PAIRS):
        at = lanes(slot * PAIRS + place, turn)
        picked = (choice == 2 * place).astype(F32).astype(BF)
        state = s_in[tile(place), :]
        adj = a_in[tile(place), :]
        dots[place : place + 1, :] = jnp.sum(adj * state, axis=0, keepdims=True)
        gw = g[:, at].astype(F32) * spread(ec, place, left)
        role = role + dot_split(gw * dot(c_bf, state.astype(BF)), picked)
        add = dot(b_bf, adj.astype(BF)) * spread(end, place, left)
        store(place, ((u[:, at] + add) * spread(dt, place, left)).astype(BF))
        outer = outer + dot_split(x[:, at].astype(F32) * add, picked)
    row, col = iota((128, PART), 0), iota((128, PART), 1)
    side = ((row >= 64).astype(jnp.int32) == col % 2).astype(F32)
    both = dot_exact(dots[...], side)
    mine = iota((PAIRS, PART), 0) == iota((PAIRS, PART), 1) // 2
    meet = jnp.exp(last) * jnp.sum(jnp.where(mine, both, 0.0), axis=0, keepdims=True)
    return role, outer, meet


def outer_kernel(
    slot, turn_ref, s_in, a_in, x, g, u, c_ref, dt_ref, bc, gx_ref, role_ref, outer_ref, meet_ref, dots
):
    def store(place, value):
        gx_ref[:, tile(place)] = value

    role, outer, meet = outer_terms(slot, turn_ref[0], s_in, a_in, x, g, u, c_ref, dt_ref, bc, dots, store)
    role_ref[...] = role
    outer_ref[...] = outer
    meet_ref[...] = jnp.broadcast_to(meet, (8, PART))


def near_kernel(turn_ref, got_s, got_a, back, xw, gw, bc, ds, out, s_own, a_own):
    turn = turn_ref[0]
    inner = ds[...].astype(BF)
    grad_b = dot(inner, bc[:, 128:])
    grad_c = dot(inner, bc[:, :128], TN)
    for place in range(PAIRS):
        at = lanes(3 * PAIRS + place, turn)
        state, adj = near_states(got_s, got_a, back, place)
        s_own[tile(place), :] = state
        a_own[tile(place), :] = adj
        grad_b = grad_b + dot(xw[:, at], adj.astype(BF), NT)
        grad_c = grad_c + dot(gw[:, at], state.astype(BF), NT)
    out[:, :128] = grad_b
    out[:, 128:] = grad_c


def more_terms(turn, k, s_in, a_in, xw, gw, grad_b, grad_c):
    for place in range(PAIRS):
        grad_b = grad_b + dot(xw[:, lanes(MIRROR[k] * PAIRS + place, turn)], a_in[tile(place), :].astype(BF), NT)
        grad_c = grad_c + dot(gw[:, lanes(k * PAIRS + place, turn)], s_in[tile(place), :].astype(BF), NT)
    return grad_b, grad_c


def middle_kernel(turn_ref, s_0, a_0, s_1, a_1, xw, gw, near, out):
    turn = turn_ref[0]
    grads = near[:, :128], near[:, 128:]
    grads = more_terms(turn, 0, s_0, a_0, xw, gw, *grads)
    grads = more_terms(turn, 1, s_1, a_1, xw, gw, *grads)
    out[:, :128] = grads[0]
    out[:, 128:] = grads[1]


def far_kernel(turn_ref, s_in, a_in, xw, gw, near, out):
    grad_b, grad_c = more_terms(turn_ref[0], 2, s_in, a_in, xw, gw, near[:, :128], near[:, 128:])
    out[:, :128] = grad_b.astype(BF).astype(F32)
    out[:, 128:] = grad_c.astype(BF).astype(F32)


def weight_kernel(tok, *refs):
    grads, rates, msg = refs[:8], refs[8], refs[9]
    total = jnp.zeros((512, 256), F32)
    for k in range(8):
        total = total + dot(tok[k], grads[k][...].astype(BF))
    for i in range(32):
        rows = slice(16 * i, 16 * i + 16)
        msg[i, 0:16, :] = total[rows, 0:128]
        msg[i, 16:32, :] = total[rows, 128:256]
        msg[i, 32:40, :] = rates[...]


def last_kernel(msg, out):
    total = msg[0]
    for k in range(1, 32):
        total = total + msg[k]
    for k in range(8):
        out[k] = total


def finish_kernel(
    turn_ref, s_0, a_0, s_2, a_2, x, g, u, c_ref, dt_ref, bc, gx_1, role_1, outer_1, meet_1, gx_3, role_3, outer_3,
    meet_3, t_rows, s_cols, logit, rate, gx_ref, step_ref, rate_ref, dots,
):
    turn = turn_ref[0]

    def terms(slot, state, adj):
        def store(place, value):
            gx_ref[:, lanes(slot * PAIRS + place, turn)] = value

        return outer_terms(slot, turn, state, adj, x, g, u, c_ref, dt_ref, bc, dots, store)

    zero, two = terms(0, s_0, a_0), terms(2, s_2, a_2)
    for place in range(PAIRS):
        gx_ref[:, lanes(PAIRS + place, turn)] = gx_1[:, tile(place)]
        gx_ref[:, lanes(3 * PAIRS + place, turn)] = gx_3[:, tile(place)]
    dt = dt_ref[...]
    role_t = jnp.concatenate([zero[0], role_1[...], two[0], role_3[...]], axis=1) + t_rows[...].T
    outer = jnp.concatenate([zero[1], outer_1[...], two[1], outer_3[...]], axis=1)
    meet = jnp.concatenate([zero[2], meet_1[0:1, :], two[2], meet_3[0:1, :]], axis=1)
    role_s = jnp.concatenate([s_cols[k] for k in range(GROUPS)], axis=1)
    row, col = iota((ROWS, ROWS), 0), iota((ROWS, ROWS), 1)
    later = (col >= row).astype(F32)
    before = (col < row).astype(F32)
    da = dot_exact(later, role_t - role_s) + dot_exact(before, outer * dt) + meet
    ddt = turned(role_s / dt + outer, turn) - rate[...] * turned(da, turn)
    step_ref[...] = ddt.T / (1.0 + jnp.exp(-logit[...]))
    rate_row = turned(-jnp.sum(dt * da, axis=0, keepdims=True), turn)
    wide = jnp.concatenate([rate_row, jnp.zeros((1, 128 - HEADS), F32)], axis=1)
    rate_ref[...] = jnp.broadcast_to(wide, (8, 128))


def shards(layer_input, projection, ssm_input, step_logit, decay_rate, output_grad):
    tok, x, g, logit = layer_input[0], ssm_input[0], output_grad[0], step_logit[0].T
    rate = decay_rate[None, :]
    width = x.shape[1]
    turn = jnp.stack([lax.axis_index(name) for name in ("turn", "y", "c")]).astype(jnp.int32)
    swap = [(0, 1), (1, 0)]
    around = [[(i, (i + hop) % 4) for i in range(4)] for hop in range(4)]
    up = [(i, i + 1) for i in range(31)]
    down = [(i + 1, i) for i in range(31)]

    bc, c, dt, rows, xw, send_s = call(
        project_kernel,
        (
            shape(ROWS, 256, dtype=BF),
            shape(ROWS, HEADS),
            shape(ROWS, HEADS),
            shape(ALL_PAIRS, 128),
            shape(ROWS, width, dtype=BF),
            shape(TILE + PAIRS, 128),
        ),
        400_000_000,
        6 << 20,
        room=52,
        in_specs=[SMEM, VMEM, VMEM, HBM, HBM, HBM],
        out_specs=(VMEM,) * 6,
        scratch_shapes=[
            pltpu.VMEM((ROWS, width), BF),
            pltpu.VMEM((width, 256), BF),
            pltpu.VMEM((ROWS, width), BF),
            pltpu.SemaphoreType.DMA((3, CHUNKS)),
        ],
        name="project",
    )(turn, logit, rate, tok, projection, x)
    got_s = lax.ppermute(send_s, SEQ, up)
    gw, send_a = call(
        adjoint_kernel,
        (shape(ROWS, width, dtype=BF), shape(TILE + PAIRS, 128)),
        140_000_000,
        3 << 20,
        in_specs=[SMEM] + [VMEM] * 4,
        out_specs=(VMEM,) * 2,
        name="adjoint",
    )(turn, bc, c, rows, g)
    got_a = lax.ppermute(send_a, SEQ, down)

    rest_s, rest_a, cg, dtg, ct = call(
        rest_kernel,
        (
            shape(3, TILE, 128),
            shape(3, TILE, 128),
            shape(GROUPS, ROWS, GROUP),
            shape(GROUPS, ROWS, GROUP),
            shape(HEADS, ROWS),
        ),
        200_000_000,
        6 << 20,
        in_specs=[SMEM] + [VMEM] * 5,
        out_specs=(VMEM,) * 5,
        name="rest",
    )(turn, bc, c, dt, xw, gw)
    columns = call(
        turn_kernel,
        (shape(512, ROWS),) * 8,
        1_000_000,
        3 << 20,
        in_specs=[SMEM, VMEM],
        out_specs=(VMEM,) * 8,
        scratch_shapes=[pltpu.VMEM((ROWS, ROWS), F32)],
        name="turn",
    )(turn, tok)
    tok_mine = columns[:4]
    tok_swapped = [lax.ppermute(piece, "c", swap) for piece in columns[4:]]

    wide = GROUP * 64

    def place(i, turn):
        return lax.rem(turn[0] + 3 - i // 2, SLOTS) * 2 + i % 2

    u, t_rows, s_cols, ds = call(
        intra_kernel,
        (
            shape(ROWS, width),
            shape(HEADS, ROWS),
            shape(GROUPS, ROWS, GROUP),
            shape(ROWS, ROWS),
        ),
        800_000_000,
        20 << 20,
        grid_spec=pltpu.PrefetchScalarGridSpec(
            num_scalar_prefetch=1,
            grid=(GROUPS,),
            in_specs=[
                pl.BlockSpec((ROWS, 256), lambda i, turn: (0, 0)),
                pl.BlockSpec((1, ROWS, GROUP), lambda i, turn: (i, 0, 0)),
                pl.BlockSpec((1, ROWS, GROUP), lambda i, turn: (i, 0, 0)),
                pl.BlockSpec((GROUP, ROWS), lambda i, turn: (i, 0)),
                pl.BlockSpec((ROWS, wide), lambda i, turn: (0, place(i, turn))),
                pl.BlockSpec((ROWS, wide), lambda i, turn: (0, place(i, turn))),
            ],
            out_specs=(
                pl.BlockSpec((ROWS, wide), lambda i, turn: (0, place(i, turn))),
                pl.BlockSpec((GROUP, ROWS), lambda i, turn: (i, 0)),
                pl.BlockSpec((1, ROWS, GROUP), lambda i, turn: (i, 0, 0)),
                pl.BlockSpec((ROWS, ROWS), lambda i, turn: (0, 0)),
            ),
        ),
        name="intra",
    )(turn, bc, cg, dtg, ct, x, g)
    got_s, got_a, *tok_swapped = lax.optimization_barrier((got_s, got_a, *tok_swapped))
    for k in (1, 2):
        got_s = lax.ppermute(advance("gather_s", gather_step_kernel, k, k)(rows, got_s, rest_s), SEQ, up)
        got_a = lax.ppermute(advance("gather_a", gather_step_kernel, MIRROR[k], k)(rows, got_a, rest_a), SEQ, down)
    got_s, got_a, u = lax.optimization_barrier((got_s, got_a, u))

    def columns_from(hop, after):
        one, two, _ = lax.optimization_barrier((tok_mine[hop], tok_swapped[hop], after))
        return [lax.ppermute(one, "y", around[hop]), lax.ppermute(two, "y", around[hop])]

    sent = call(
        combine_kernel,
        shape(PAIRS, 264, 128),
        4_000_000,
        4 << 20,
        in_specs=[VMEM] * 5,
        out_specs=VMEM,
        name="combine",
    )(rows, rest_s, rest_a, got_s, got_a)
    near_columns = columns_from(1, sent) + columns_from(3, sent)
    held = lax.all_to_all(sent, BLOCK, 0, 0)
    held, *near_columns = lax.optimization_barrier((held, *near_columns))
    scanned = call(
        scan_kernel,
        shape(PAIRS, 256, 128),
        4_000_000,
        4 << 20,
        in_specs=[VMEM],
        out_specs=VMEM,
        name="scan",
    )(held)
    far_columns = columns_from(2, scanned)
    back = lax.all_to_all(scanned, BLOCK, 0, 0)
    back, *far_columns = lax.optimization_barrier((back, *far_columns))
    tok_got = [tok_mine[0], tok_swapped[0], *near_columns[:2], *far_columns, *near_columns[2:]]
    s_next, a_next = call(
        unfold_kernel,
        (shape(TILE, 128),) * 2,
        8_000_000,
        4 << 20,
        in_specs=[VMEM] * 6,
        out_specs=(VMEM,) * 2,
        name="unfold",
    )(rows, rest_s, rest_a, got_s, got_a, back)
    s_0 = lax.ppermute(s_next, SEQ, up)
    a_0 = lax.ppermute(a_next, SEQ, down)
    near, s_own, a_own = call(
        near_kernel,
        (shape(ROWS, 256), shape(TILE, 128), shape(TILE, 128)),
        140_000_000,
        4 << 20,
        in_specs=[SMEM] + [VMEM] * 7,
        out_specs=(VMEM,) * 3,
        name="near",
    )(turn, got_s, got_a, back, xw, gw, bc, ds)

    def outer_part(slot, state, adj):
        return call(
            functools.partial(outer_kernel, slot),
            (
                shape(ROWS, TILE, dtype=BF),
                shape(ROWS, PART),
                shape(ROWS, PART),
                shape(8, PART),
            ),
            250_000_000,
            6 << 20,
            in_specs=[SMEM] + [VMEM] * 8,
            out_specs=(VMEM,) * 4,
            scratch_shapes=[pltpu.VMEM((PAIRS, 128), F32)],
            name="outer",
        )(turn, state, adj, x, g, u, c, dt, bc)

    own = outer_part(3, s_own, a_own)
    all_tok = call(
        narrow_kernel,
        shape(8, 512, ROWS, dtype=BF),
        1_000_000,
        3 << 20,
        in_specs=[VMEM] * 8,
        out_specs=VMEM,
        name="narrow",
    )(*tok_got)
    s_1 = lax.ppermute(advance("spread_s", spread_step_kernel, 0)(rows, s_0, send_s), SEQ, up)
    a_1 = lax.ppermute(advance("spread_a", spread_step_kernel, MIRROR[0])(rows, a_0, send_a), SEQ, down)
    s_2 = lax.ppermute(advance("spread_s", spread_rest_kernel, 1)(rows, s_1, rest_s), SEQ, up)
    a_2 = lax.ppermute(advance("spread_a", spread_rest_kernel, MIRROR[1])(rows, a_1, rest_a), SEQ, down)
    middle = call(
        middle_kernel,
        shape(ROWS, 256),
        140_000_000,
        4 << 20,
        in_specs=[SMEM] + [VMEM] * 7,
        out_specs=VMEM,
        name="middle",
    )(turn, s_0, a_0, s_1, a_1, xw, gw, near)
    one = outer_part(1, s_1, a_1)
    s_2, a_2, middle, one, own, all_tok = lax.optimization_barrier((s_2, a_2, middle, one, own, all_tok))
    part = call(
        far_kernel,
        shape(ROWS, 256),
        70_000_000,
        3 << 20,
        in_specs=[SMEM] + [VMEM] * 5,
        out_specs=VMEM,
        name="far",
    )(turn, s_2, a_2, xw, gw, middle)
    mine = [part] + [lax.ppermute(part, "y", around[hop]) for hop in (1, 2, 3)]
    other = [lax.ppermute(piece, "c", swap) for piece in mine]
    gx, step_grad, rates = call(
        finish_kernel,
        (shape(ROWS, width, dtype=BF), shape(HEADS, ROWS), shape(8, 128)),
        500_000_000,
        6 << 20,
        in_specs=[SMEM] + [VMEM] * 22,
        out_specs=(VMEM,) * 3,
        scratch_shapes=[pltpu.VMEM((PAIRS, 128), F32)],
        name="finish",
    )(turn, s_0, a_2, s_2, a_0, x, g, u, c, dt, bc, *one, *own, t_rows, s_cols, logit, rate)
    grads = [piece for pair in zip(mine, other) for piece in pair]
    weight = call(
        weight_kernel,
        shape(32, 40, 128),
        300_000_000,
        3 << 20,
        in_specs=[VMEM] * 10,
        out_specs=VMEM,
        name="weight",
    )(all_tok, *grads, rates)
    summed = call(
        last_kernel,
        shape(8, 40, 128),
        1_000_000,
        1 << 20,
        in_specs=[VMEM],
        out_specs=VMEM,
        name="last",
    )(lax.all_to_all(weight, SEQ, 0, 0))
    last = lax.all_to_all(summed, ("y", "c"), 0, 0)
    full = jnp.concatenate([last[:, :16].reshape(ROWS, 128), last[:, 16:32].reshape(ROWS, 128)], axis=1)
    return gx[None], step_grad.T[None], jnp.sum(last[:, 32, :HEADS], axis=0), full


def solution(mesh):
    devices = mesh.devices.reshape(4, 2, 4, 4, 2)
    parts = Mesh(devices, ("x", "quad", "turn", "y", "c"))
    rows = P(("y", "c"), SEQ, None)
    return jax.shard_map(
        shards,
        mesh=parts,
        in_specs=(rows, P(), rows, rows, P(), rows),
        out_specs=(rows, rows, P(), P(SEQ, None)),
        check_vma=False,
    )
```

```python
import functools

import jax
import jax.numpy as jnp
from jax import lax
from jax.experimental import pallas as pl
from jax.experimental.pallas import tpu as pltpu
from jax.sharding import Mesh
from jax.sharding import PartitionSpec as P

ROWS = 128
HEADS = 64
SLOTS = 4
PART = HEADS // SLOTS
PAIRS = PART // 2
ALL_PAIRS = HEADS // 2
TILE = PAIRS * 128
MIRROR = (2, 1, 0, 3)
GROUP = 8
GROUPS = HEADS // GROUP
BF = jnp.bfloat16
F32 = jnp.float32
NN = (((1,), (0,)), ((), ()))
NT = (((1,), (1,)), ((), ()))
TN = (((0,), (0,)), ((), ()))
HIGH = lax.Precision.HIGHEST
VMEM = pl.BlockSpec(memory_space=pltpu.VMEM)
SMEM = pl.BlockSpec(memory_space=pltpu.SMEM)
HBM = pl.BlockSpec(memory_space=pltpu.HBM)
SEQ = ("x", "quad", "turn")
BLOCK = ("x", "quad")
CHUNKS = 4
CHUNK = 1024


def iota(shape, dim):
    return lax.broadcasted_iota(jnp.int32, shape, dim)


def dot(a, b, dims=NN):
    return lax.dot_general(a, b, dims, preferred_element_type=F32)


def dot_exact(a, b):
    return lax.dot_general(a, b, NN, precision=HIGH, preferred_element_type=F32)


def dot_split(a, b):
    head = a.astype(BF)
    tail = (a - head.astype(F32)).astype(BF)
    return dot(head, b) + dot(tail, b)


def spread(cols, pair, left):
    one = cols[:, 2 * pair : 2 * pair + 1]
    two = cols[:, 2 * pair + 1 : 2 * pair + 2]
    return jnp.where(left, one, two)


def turned(values, turn):
    parts = [values[:, PART * k : PART * k + PART] for k in range(SLOTS)]
    out = values
    for t in range(SLOTS):
        order = jnp.concatenate([parts[(t + 3 - k) % SLOTS] for k in range(SLOTS)], axis=1)
        out = jnp.where(turn == t, order, out)
    return out


def lanes(pair, turn):
    slot, place = divmod(pair, PAIRS)
    start = lax.rem(turn + 3 - slot, SLOTS) * TILE + 128 * place
    return pl.ds(pl.multiple_of(start, 128), 128)


def tile(place):
    return slice(128 * place, 128 * place + 128)


def call(kernel, outs, flops, moved, room=8, **more):
    return pl.pallas_call(
        kernel,
        out_shape=outs,
        compiler_params=pltpu.CompilerParams(vmem_limit_bytes=room << 20),
        cost_estimate=pl.CostEstimate(flops=flops, bytes_accessed=moved, transcendentals=0),
        **more,
    )


def shape(*dims, dtype=F32):
    return jax.ShapeDtypeStruct(dims, dtype)


def advance(name, kernel, *fixed):
    return call(
        functools.partial(kernel, *fixed),
        shape(TILE + PAIRS if kernel is gather_step_kernel else TILE, 128),
        1_000_000,
        2 << 20,
        in_specs=[VMEM] * 3,
        out_specs=VMEM,
        name=name,
    )


def turn_kernel(place_ref, tok, *refs):
    y, core = place_ref[1], place_ref[2]
    outs, held = refs[:8], refs[8]
    for i in range(32):
        held[...] = tok[:, tile(i)].astype(F32).T
        for hop in range(4):
            for side in range(2):
                start = lax.rem(y + hop, 4) * 32 + lax.rem(core + side, 2) * 16
                outs[4 * side + hop][16 * i : 16 * i + 16, :] = held[pl.ds(pl.multiple_of(start, 16), 16), :]


def narrow_kernel(*refs):
    for k in range(8):
        refs[8][k] = refs[k][...].astype(BF)


def project_kernel(
    turn_ref, logit, rate, tok_hbm, proj_hbm, x_hbm, bc_ref, c_ref, dt_ref, rows_ref, xw_ref, send, tok, proj, x, sems
):
    copies = []
    for k in range(CHUNKS):
        at = pl.ds(k * CHUNK, CHUNK)
        copies.append(
            (
                pltpu.make_async_copy(tok_hbm.at[:, at], tok.at[:, at], sems.at[0, k]),
                pltpu.make_async_copy(proj_hbm.at[at, :], proj.at[at, :], sems.at[1, k]),
            )
        )
        for copy in copies[-1]:
            copy.start()
    fetch_x = pltpu.make_async_copy(x_hbm, x, sems.at[2, 0])
    fetch_x.start()
    turn = turn_ref[0]
    z = turned(logit[...].T, turn)
    dt = jnp.maximum(z, 0.0) + jnp.log1p(jnp.exp(-jnp.abs(z)))
    a = -turned(rate[...], turn) * dt
    lower = (iota((ROWS, ROWS), 0) >= iota((ROWS, ROWS), 1)).astype(F32)
    c = dot_exact(lower, a)
    c_ref[...] = c
    dt_ref[...] = dt
    last = c[ROWS - 1 : ROWS, :]
    to_end = jnp.exp(last - c) * dt
    left = iota((ROWS, 128), 1) < 64
    left1 = iota((1, 128), 1) < 64
    for pair in range(ALL_PAIRS):
        rows_ref[pair : pair + 1, :] = spread(last, pair, left1)
    send[TILE : TILE + PAIRS, :] = rows_ref[0:PAIRS, :]
    total = jnp.zeros((ROWS, 256), F32)
    for k in range(CHUNKS):
        for copy in copies[k]:
            copy.wait()
        at = slice(k * CHUNK, k * CHUNK + CHUNK)
        total = total + dot(tok[:, at], proj[at, :])
    bc = total.astype(BF)
    bc_ref[...] = bc
    b_t = bc[:, :128].astype(F32).T.astype(BF)
    fetch_x.wait()
    for pair in range(ALL_PAIRS):
        at = lanes(pair, turn)
        xw = (x[:, at].astype(F32) * spread(to_end, pair, left)).astype(BF)
        xw_ref[:, at] = xw
        if pair < PAIRS:
            send[tile(pair), :] = dot(b_t, xw)


def adjoint_kernel(turn_ref, bc, c_ref, rows, g, gw_ref, send):
    turn = turn_ref[0]
    ec = jnp.exp(c_ref[...])
    c_t = bc[:, 128:].astype(F32).T.astype(BF)
    left = iota((ROWS, 128), 1) < 64
    first = MIRROR[0] * PAIRS
    for pair in range(ALL_PAIRS):
        at = lanes(pair, turn)
        gw = (g[:, at].astype(F32) * spread(ec, pair, left)).astype(BF)
        gw_ref[:, at] = gw
        if first <= pair < first + PAIRS:
            send[tile(pair - first), :] = dot(c_t, gw)
    send[TILE : TILE + PAIRS, :] = rows[first : first + PAIRS, :]


def rest_kernel(turn_ref, bc, c_ref, dt_ref, xw, gw, rest_s, rest_a, cg_ref, dtg_ref, ct_ref):
    turn = turn_ref[0]
    both = bc[...].astype(F32)
    b_t = both[:, :128].T.astype(BF)
    c_t = both[:, 128:].T.astype(BF)
    for k in range(1, SLOTS):
        for place in range(PAIRS):
            rest_s[k - 1, tile(place), :] = dot(b_t, xw[:, lanes(k * PAIRS + place, turn)])
            rest_a[k - 1, tile(place), :] = dot(c_t, gw[:, lanes(MIRROR[k] * PAIRS + place, turn)])
    c = c_ref[...]
    ct_ref[...] = c.T
    for group in range(GROUPS):
        cg_ref[group] = c[:, GROUP * group : GROUP * group + GROUP]
        dtg_ref[group] = dt_ref[:, GROUP * group : GROUP * group + GROUP]


def gather_step_kernel(slot, k, rows, got, rest, out):
    for place in range(PAIRS):
        own = rows[slot * PAIRS + place : slot * PAIRS + place + 1, :]
        out[tile(place), :] = jnp.exp(own) * got[tile(place), :] + rest[k - 1, tile(place), :]
    out[TILE : TILE + PAIRS, :] = got[TILE : TILE + PAIRS, :] + rows[slot * PAIRS : slot * PAIRS + PAIRS, :]


def spread_step_kernel(slot, rows, state, local, out):
    for place in range(PAIRS):
        own = rows[slot * PAIRS + place : slot * PAIRS + place + 1, :]
        out[tile(place), :] = jnp.exp(own) * state[tile(place), :] + local[tile(place), :]


def spread_rest_kernel(slot, rows, state, rest, out):
    spread_step_kernel(slot, rows, state, rest.at[0], out)


def intra_kernel(turn_ref, bc, cg, dtg, ct, x, g, u_ref, t_ref, s_ref, ds_ref):
    @pl.when(pl.program_id(0) == 0)
    def _():
        ds_ref[...] = jnp.zeros_like(ds_ref)

    sc_t = dot(bc[:, :128], bc[:, 128:], NT)
    causal = iota((ROWS, ROWS), 0) <= iota((ROWS, ROWS), 1)
    left = iota((ROWS, 128), 1) < 64
    ones = (left.astype(F32).astype(BF), (1.0 - left.astype(F32)).astype(BF))
    lane8 = iota((ROWS, GROUP), 1)
    s_all = jnp.zeros((ROWS, GROUP), F32)
    total = ds_ref[...]
    for pair in range(GROUP // 2):
        xs = x[:, 128 * pair : 128 * pair + 128]
        gs = g[:, 128 * pair : 128 * pair + 128]
        parts = []
        for side in range(2):
            h = 2 * pair + side
            gx = dot(xs * ones[side], gs, NT)
            gap = ct[h : h + 1, :] - cg[0, :, h : h + 1]
            decay = jnp.exp(jnp.where(causal, gap, -jnp.inf))
            parts.append(dot((decay * sc_t).astype(BF), gs))
            p = decay * gx * dtg[0, :, h : h + 1]
            total = total + p
            m = p * sc_t
            t_ref[h : h + 1, :] = jnp.sum(m, axis=0, keepdims=True)
            s_all = jnp.where(lane8 == h, jnp.sum(m, axis=1, keepdims=True), s_all)
        u_ref[:, 128 * pair : 128 * pair + 128] = jnp.where(left, parts[0], parts[1])
    s_ref[0] = s_all
    ds_ref[...] = total


def combine_kernel(rows, rest_s, rest_a, got_s, got_a, msg):
    for place in range(PAIRS):
        own = rows[3 * PAIRS + place : 3 * PAIRS + place + 1, :]
        decay = jnp.exp(own)
        msg[place, 0:128, :] = decay * got_s[tile(place), :] + rest_s[2, tile(place), :]
        msg[place, 128:256, :] = decay * got_a[tile(place), :] + rest_a[2, tile(place), :]
        msg[place, 256:257, :] = own + got_s[TILE + place : TILE + place + 1, :]
        msg[place, 257:258, :] = own + got_a[TILE + place : TILE + place + 1, :]
        msg[place, 258:264, :] = jnp.zeros((6, 128), F32)


def scan_kernel(msg, out):
    state = jnp.zeros((128, 128), F32)
    for i in range(PAIRS):
        out[i, 0:128, :] = state
        state = jnp.exp(msg[i, 256:257, :]) * state + msg[i, 0:128, :]
    state = jnp.zeros((128, 128), F32)
    for i in range(PAIRS - 1, -1, -1):
        out[i, 128:256, :] = state
        state = jnp.exp(msg[i, 257:258, :]) * state + msg[i, 128:256, :]


def near_states(got_s, got_a, back, place):
    mark = TILE + place
    state = jnp.exp(got_s[mark : mark + 1, :]) * back[place, 0:128, :] + got_s[tile(place), :]
    adj = jnp.exp(got_a[mark : mark + 1, :]) * back[place, 128:256, :] + got_a[tile(place), :]
    return state, adj


def unfold_kernel(rows, rest_s, rest_a, got_s, got_a, back, s_next, a_next):
    for place in range(PAIRS):
        state, adj = near_states(got_s, got_a, back, place)
        decay = jnp.exp(rows[3 * PAIRS + place : 3 * PAIRS + place + 1, :])
        s_next[tile(place), :] = decay * state + rest_s[2, tile(place), :]
        a_next[tile(place), :] = decay * adj + rest_a[2, tile(place), :]


def outer_terms(slot, turn, s_in, a_in, x, g, u, c_ref, dt_ref, bc, dots, store):
    cols = slice(PART * slot, PART * slot + PART)
    c = c_ref[:, cols]
    dt = dt_ref[:, cols]
    last = c[ROWS - 1 : ROWS, :]
    end = jnp.exp(last - c)
    ec = jnp.exp(c)
    b_bf, c_bf = bc[:, :128], bc[:, 128:]
    left = iota((ROWS, 128), 1) < 64
    choice = iota((ROWS, PART), 1) - (iota((ROWS, PART), 0) >= 64).astype(jnp.int32)
    role = jnp.zeros((ROWS, PART), F32)
    outer = jnp.zeros((ROWS, PART), F32)
    for place in range(PAIRS):
        at = lanes(slot * PAIRS + place, turn)
        picked = (choice == 2 * place).astype(F32).astype(BF)
        state = s_in[tile(place), :]
        adj = a_in[tile(place), :]
        dots[place : place + 1, :] = jnp.sum(adj * state, axis=0, keepdims=True)
        gw = g[:, at].astype(F32) * spread(ec, place, left)
        role = role + dot_split(gw * dot(c_bf, state.astype(BF)), picked)
        add = dot(b_bf, adj.astype(BF)) * spread(end, place, left)
        store(place, ((u[:, at] + add) * spread(dt, place, left)).astype(BF))
        outer = outer + dot_split(x[:, at].astype(F32) * add, picked)
    row, col = iota((128, PART), 0), iota((128, PART), 1)
    side = ((row >= 64).astype(jnp.int32) == col % 2).astype(F32)
    both = dot_exact(dots[...], side)
    mine = iota((PAIRS, PART), 0) == iota((PAIRS, PART), 1) // 2
    meet = jnp.exp(last) * jnp.sum(jnp.where(mine, both, 0.0), axis=0, keepdims=True)
    return role, outer, meet


def outer_kernel(
    slot, turn_ref, s_in, a_in, x, g, u, c_ref, dt_ref, bc, gx_ref, role_ref, outer_ref, meet_ref, dots
):
    def store(place, value):
        gx_ref[:, tile(place)] = value

    role, outer, meet = outer_terms(slot, turn_ref[0], s_in, a_in, x, g, u, c_ref, dt_ref, bc, dots, store)
    role_ref[...] = role
    outer_ref[...] = outer
    meet_ref[...] = jnp.broadcast_to(meet, (8, PART))


def near_kernel(turn_ref, got_s, got_a, back, xw, gw, bc, ds, out, s_own, a_own):
    turn = turn_ref[0]
    inner = ds[...].astype(BF)
    grad_b = dot(inner, bc[:, 128:])
    grad_c = dot(inner, bc[:, :128], TN)
    for place in range(PAIRS):
        at = lanes(3 * PAIRS + place, turn)
        state, adj = near_states(got_s, got_a, back, place)
        s_own[tile(place), :] = state
        a_own[tile(place), :] = adj
        grad_b = grad_b + dot(xw[:, at], adj.astype(BF), NT)
        grad_c = grad_c + dot(gw[:, at], state.astype(BF), NT)
    out[:, :128] = grad_b
    out[:, 128:] = grad_c


def more_terms(turn, k, s_in, a_in, xw, gw, grad_b, grad_c):
    for place in range(PAIRS):
        grad_b = grad_b + dot(xw[:, lanes(MIRROR[k] * PAIRS + place, turn)], a_in[tile(place), :].astype(BF), NT)
        grad_c = grad_c + dot(gw[:, lanes(k * PAIRS + place, turn)], s_in[tile(place), :].astype(BF), NT)
    return grad_b, grad_c


def middle_kernel(turn_ref, s_0, a_0, s_1, a_1, xw, gw, near, out):
    turn = turn_ref[0]
    grads = near[:, :128], near[:, 128:]
    grads = more_terms(turn, 0, s_0, a_0, xw, gw, *grads)
    grads = more_terms(turn, 1, s_1, a_1, xw, gw, *grads)
    out[:, :128] = grads[0]
    out[:, 128:] = grads[1]


def far_kernel(turn_ref, s_in, a_in, xw, gw, near, out):
    grad_b, grad_c = more_terms(turn_ref[0], 2, s_in, a_in, xw, gw, near[:, :128], near[:, 128:])
    out[:, :128] = grad_b.astype(BF).astype(F32)
    out[:, 128:] = grad_c.astype(BF).astype(F32)


def weight_kernel(tok, *refs):
    grads, rates, msg = refs[:8], refs[8], refs[9]
    total = jnp.zeros((512, 256), F32)
    for k in range(8):
        total = total + dot(tok[k], grads[k][...].astype(BF))
    for i in range(32):
        rows = slice(16 * i, 16 * i + 16)
        msg[i, 0:16, :] = total[rows, 0:128]
        msg[i, 16:32, :] = total[rows, 128:256]
        msg[i, 32:40, :] = rates[...]


def last_kernel(msg, out):
    total = msg[0]
    for k in range(1, 32):
        total = total + msg[k]
    for k in range(8):
        out[k] = total


def finish_kernel(
    turn_ref, s_0, a_0, s_2, a_2, x, g, u, c_ref, dt_ref, bc, gx_1, role_1, outer_1, meet_1, gx_3, role_3, outer_3,
    meet_3, t_rows, s_cols, logit, rate, gx_ref, step_ref, rate_ref, dots,
):
    turn = turn_ref[0]

    def terms(slot, state, adj):
        def store(place, value):
            gx_ref[:, lanes(slot * PAIRS + place, turn)] = value

        return outer_terms(slot, turn, state, adj, x, g, u, c_ref, dt_ref, bc, dots, store)

    zero, two = terms(0, s_0, a_0), terms(2, s_2, a_2)
    for place in range(PAIRS):
        gx_ref[:, lanes(PAIRS + place, turn)] = gx_1[:, tile(place)]
        gx_ref[:, lanes(3 * PAIRS + place, turn)] = gx_3[:, tile(place)]
    dt = dt_ref[...]
    role_t = jnp.concatenate([zero[0], role_1[...], two[0], role_3[...]], axis=1) + t_rows[...].T
    outer = jnp.concatenate([zero[1], outer_1[...], two[1], outer_3[...]], axis=1)
    meet = jnp.concatenate([zero[2], meet_1[0:1, :], two[2], meet_3[0:1, :]], axis=1)
    role_s = jnp.concatenate([s_cols[k] for k in range(GROUPS)], axis=1)
    row, col = iota((ROWS, ROWS), 0), iota((ROWS, ROWS), 1)
    later = (col >= row).astype(F32)
    before = (col < row).astype(F32)
    da = dot_exact(later, role_t - role_s) + dot_exact(before, outer * dt) + meet
    ddt = turned(role_s / dt + outer, turn) - rate[...] * turned(da, turn)
    step_ref[...] = ddt.T / (1.0 + jnp.exp(-logit[...]))
    rate_row = turned(-jnp.sum(dt * da, axis=0, keepdims=True), turn)
    wide = jnp.concatenate([rate_row, jnp.zeros((1, 128 - HEADS), F32)], axis=1)
    rate_ref[...] = jnp.broadcast_to(wide, (8, 128))


def shards(layer_input, projection, ssm_input, step_logit, decay_rate, output_grad):
    tok, x, g, logit = layer_input[0], ssm_input[0], output_grad[0], step_logit[0].T
    rate = decay_rate[None, :]
    width = x.shape[1]
    turn = jnp.stack([lax.axis_index(name) for name in ("turn", "y", "c")]).astype(jnp.int32)
    swap = [(0, 1), (1, 0)]
    around = [[(i, (i + hop) % 4) for i in range(4)] for hop in range(4)]
    up = [(i, i + 1) for i in range(31)]
    down = [(i + 1, i) for i in range(31)]

    bc, c, dt, rows, xw, send_s = call(
        project_kernel,
        (
            shape(ROWS, 256, dtype=BF),
            shape(ROWS, HEADS),
            shape(ROWS, HEADS),
            shape(ALL_PAIRS, 128),
            shape(ROWS, width, dtype=BF),
            shape(TILE + PAIRS, 128),
        ),
        400_000_000,
        6 << 20,
        room=52,
        in_specs=[SMEM, VMEM, VMEM, HBM, HBM, HBM],
        out_specs=(VMEM,) * 6,
        scratch_shapes=[
            pltpu.VMEM((ROWS, width), BF),
            pltpu.VMEM((width, 256), BF),
            pltpu.VMEM((ROWS, width), BF),
            pltpu.SemaphoreType.DMA((3, CHUNKS)),
        ],
        name="project",
    )(turn, logit, rate, tok, projection, x)
    got_s = lax.ppermute(send_s, SEQ, up)
    gw, send_a = call(
        adjoint_kernel,
        (shape(ROWS, width, dtype=BF), shape(TILE + PAIRS, 128)),
        140_000_000,
        3 << 20,
        in_specs=[SMEM] + [VMEM] * 4,
        out_specs=(VMEM,) * 2,
        name="adjoint",
    )(turn, bc, c, rows, g)
    got_a = lax.ppermute(send_a, SEQ, down)

    rest_s, rest_a, cg, dtg, ct = call(
        rest_kernel,
        (
            shape(3, TILE, 128),
            shape(3, TILE, 128),
            shape(GROUPS, ROWS, GROUP),
            shape(GROUPS, ROWS, GROUP),
            shape(HEADS, ROWS),
        ),
        200_000_000,
        6 << 20,
        in_specs=[SMEM] + [VMEM] * 5,
        out_specs=(VMEM,) * 5,
        name="rest",
    )(turn, bc, c, dt, xw, gw)
    columns = call(
        turn_kernel,
        (shape(512, ROWS),) * 8,
        1_000_000,
        3 << 20,
        in_specs=[SMEM, VMEM],
        out_specs=(VMEM,) * 8,
        scratch_shapes=[pltpu.VMEM((ROWS, ROWS), F32)],
        name="turn",
    )(turn, tok)
    tok_mine = columns[:4]
    tok_swapped = [lax.ppermute(piece, "c", swap) for piece in columns[4:]]

    wide = GROUP * 64

    def place(i, turn):
        return lax.rem(turn[0] + 3 - i // 2, SLOTS) * 2 + i % 2

    u, t_rows, s_cols, ds = call(
        intra_kernel,
        (
            shape(ROWS, width),
            shape(HEADS, ROWS),
            shape(GROUPS, ROWS, GROUP),
            shape(ROWS, ROWS),
        ),
        800_000_000,
        20 << 20,
        grid_spec=pltpu.PrefetchScalarGridSpec(
            num_scalar_prefetch=1,
            grid=(GROUPS,),
            in_specs=[
                pl.BlockSpec((ROWS, 256), lambda i, turn: (0, 0)),
                pl.BlockSpec((1, ROWS, GROUP), lambda i, turn: (i, 0, 0)),
                pl.BlockSpec((1, ROWS, GROUP), lambda i, turn: (i, 0, 0)),
                pl.BlockSpec((GROUP, ROWS), lambda i, turn: (i, 0)),
                pl.BlockSpec((ROWS, wide), lambda i, turn: (0, place(i, turn))),
                pl.BlockSpec((ROWS, wide), lambda i, turn: (0, place(i, turn))),
            ],
            out_specs=(
                pl.BlockSpec((ROWS, wide), lambda i, turn: (0, place(i, turn))),
                pl.BlockSpec((GROUP, ROWS), lambda i, turn: (i, 0)),
                pl.BlockSpec((1, ROWS, GROUP), lambda i, turn: (i, 0, 0)),
                pl.BlockSpec((ROWS, ROWS), lambda i, turn: (0, 0)),
            ),
        ),
        name="intra",
    )(turn, bc, cg, dtg, ct, x, g)
    got_s, got_a, *tok_swapped = lax.optimization_barrier((got_s, got_a, *tok_swapped))
    for k in (1, 2):
        got_s = lax.ppermute(advance("gather_s", gather_step_kernel, k, k)(rows, got_s, rest_s), SEQ, up)
        got_a = lax.ppermute(advance("gather_a", gather_step_kernel, MIRROR[k], k)(rows, got_a, rest_a), SEQ, down)
    got_s, got_a, u = lax.optimization_barrier((got_s, got_a, u))

    def columns_from(hop, after):
        one, two, _ = lax.optimization_barrier((tok_mine[hop], tok_swapped[hop], after))
        return [lax.ppermute(one, "y", around[hop]), lax.ppermute(two, "y", around[hop])]

    sent = call(
        combine_kernel,
        shape(PAIRS, 264, 128),
        4_000_000,
        4 << 20,
        in_specs=[VMEM] * 5,
        out_specs=VMEM,
        name="combine",
    )(rows, rest_s, rest_a, got_s, got_a)
    near_columns = columns_from(1, sent) + columns_from(3, sent)
    held = lax.all_to_all(sent, BLOCK, 0, 0)
    held, *near_columns = lax.optimization_barrier((held, *near_columns))
    scanned = call(
        scan_kernel,
        shape(PAIRS, 256, 128),
        4_000_000,
        4 << 20,
        in_specs=[VMEM],
        out_specs=VMEM,
        name="scan",
    )(held)
    back = lax.all_to_all(scanned, BLOCK, 0, 0)
    s_next, a_next = call(
        unfold_kernel,
        (shape(TILE, 128),) * 2,
        8_000_000,
        4 << 20,
        in_specs=[VMEM] * 6,
        out_specs=(VMEM,) * 2,
        name="unfold",
    )(rows, rest_s, rest_a, got_s, got_a, back)
    s_0 = lax.ppermute(s_next, SEQ, up)
    a_0 = lax.ppermute(a_next, SEQ, down)
    far_columns = columns_from(2, s_next)
    near, s_own, a_own = call(
        near_kernel,
        (shape(ROWS, 256), shape(TILE, 128), shape(TILE, 128)),
        140_000_000,
        4 << 20,
        in_specs=[SMEM] + [VMEM] * 7,
        out_specs=(VMEM,) * 3,
        name="near",
    )(turn, got_s, got_a, back, xw, gw, bc, ds)

    def outer_part(slot, state, adj):
        return call(
            functools.partial(outer_kernel, slot),
            (
                shape(ROWS, TILE, dtype=BF),
                shape(ROWS, PART),
                shape(ROWS, PART),
                shape(8, PART),
            ),
            250_000_000,
            6 << 20,
            in_specs=[SMEM] + [VMEM] * 8,
            out_specs=(VMEM,) * 4,
            scratch_shapes=[pltpu.VMEM((PAIRS, 128), F32)],
            name="outer",
        )(turn, state, adj, x, g, u, c, dt, bc)

    own = outer_part(3, s_own, a_own)
    s_1 = lax.ppermute(advance("spread_s", spread_step_kernel, 0)(rows, s_0, send_s), SEQ, up)
    a_1 = lax.ppermute(advance("spread_a", spread_step_kernel, MIRROR[0])(rows, a_0, send_a), SEQ, down)
    s_1, a_1, *far_columns = lax.optimization_barrier((s_1, a_1, *far_columns))
    tok_got = [tok_mine[0], tok_swapped[0], *near_columns[:2], *far_columns, *near_columns[2:]]
    all_tok = call(
        narrow_kernel,
        shape(8, 512, ROWS, dtype=BF),
        1_000_000,
        3 << 20,
        in_specs=[VMEM] * 8,
        out_specs=VMEM,
        name="narrow",
    )(*tok_got)
    s_2 = lax.ppermute(advance("spread_s", spread_rest_kernel, 1)(rows, s_1, rest_s), SEQ, up)
    a_2 = lax.ppermute(advance("spread_a", spread_rest_kernel, MIRROR[1])(rows, a_1, rest_a), SEQ, down)
    middle = call(
        middle_kernel,
        shape(ROWS, 256),
        140_000_000,
        4 << 20,
        in_specs=[SMEM] + [VMEM] * 7,
        out_specs=VMEM,
        name="middle",
    )(turn, s_0, a_0, s_1, a_1, xw, gw, near)
    one = outer_part(1, s_1, a_1)
    s_2, a_2, middle, one, own, all_tok = lax.optimization_barrier((s_2, a_2, middle, one, own, all_tok))
    part = call(
        far_kernel,
        shape(ROWS, 256),
        70_000_000,
        3 << 20,
        in_specs=[SMEM] + [VMEM] * 5,
        out_specs=VMEM,
        name="far",
    )(turn, s_2, a_2, xw, gw, middle)
    mine = [part] + [lax.ppermute(part, "y", around[hop]) for hop in (1, 2, 3)]
    other = [lax.ppermute(piece, "c", swap) for piece in mine]
    gx, step_grad, rates = call(
        finish_kernel,
        (shape(ROWS, width, dtype=BF), shape(HEADS, ROWS), shape(8, 128)),
        500_000_000,
        6 << 20,
        in_specs=[SMEM] + [VMEM] * 22,
        out_specs=(VMEM,) * 3,
        scratch_shapes=[pltpu.VMEM((PAIRS, 128), F32)],
        name="finish",
    )(turn, s_0, a_2, s_2, a_0, x, g, u, c, dt, bc, *one, *own, t_rows, s_cols, logit, rate)
    grads = [piece for pair in zip(mine, other) for piece in pair]
    weight = call(
        weight_kernel,
        shape(32, 40, 128),
        300_000_000,
        3 << 20,
        in_specs=[VMEM] * 10,
        out_specs=VMEM,
        name="weight",
    )(all_tok, *grads, rates)
    summed = call(
        last_kernel,
        shape(8, 40, 128),
        1_000_000,
        1 << 20,
        in_specs=[VMEM],
        out_specs=VMEM,
        name="last",
    )(lax.all_to_all(weight, SEQ, 0, 0))
    last = lax.all_to_all(summed, ("y", "c"), 0, 0)
    full = jnp.concatenate([last[:, :16].reshape(ROWS, 128), last[:, 16:32].reshape(ROWS, 128)], axis=1)
    return gx[None], step_grad.T[None], jnp.sum(last[:, 32, :HEADS], axis=0), full


def solution(mesh):
    devices = mesh.devices.reshape(4, 2, 4, 4, 2)
    parts = Mesh(devices, ("x", "quad", "turn", "y", "c"))
    rows = P(("y", "c"), SEQ, None)
    return jax.shard_map(
        shards,
        mesh=parts,
        in_specs=(rows, P(), rows, rows, P(), rows),
        out_specs=(rows, rows, P(), P(SEQ, None)),
        check_vma=False,
    )
```
